256 devices in a mesh: leaf: 4 (over y), col: 64 (over x, z, core).
Axes of the slice: x: 4, y: 4, z: 8, core: 2. Of those that a mesh axis runs over, the one named last changes fastest.
Arguments:
- node_rhs: float32 [4, 64, 9, 256, 256], P('leaf', 'col'), may hold values from -0.125 to 0.125
- node_inverse: float32 [4, 64, 9, 256, 256], P('leaf', 'col')
- local_blocks: float32 [4, 64, 8, 2, 64, 256], P('leaf', 'col'), may hold values from -0.09375 to 0.09375
- chain_next: float32 [4, 64, 256, 256], P('leaf', 'col')
- chain_top: float32 [4, 64, 64, 256], P('leaf', 'col'), may hold values from -0.09375 to 0.09375
- top_rhs: float32 [4, 256, 256], replicated, may hold values from -6 to 6
- top_inverse: float32 [4, 256, 256], replicated
- top_next: float32 [3, 256, 256], replicated, may hold values from -0.1875 to 0.1875
- ancestors: int32 [4, 64, 8, 2], P('leaf', 'col'), may hold values from 0 to 8, as said below
- block_rows: int32 [4, 64, 8, 2, 64], P('leaf', 'col'), may hold values from 0 to 255, as said below
- chain_target: int32 [4, 64], P('leaf', 'col'), may hold values from 0 to 3
- chain_rows: int32 [4, 64, 64], P('leaf', 'col'), may hold values from 0 to 255, as said below
Outputs:
- node_solution: float32 [4, 64, 9, 256, 256], P('leaf', 'col')
- top_solution: float32 [4, 256, 256], replicated
The draws below stay inside these ranges and needn't reach their ends.
Inputs may be any that keep to these rules, and one draw needn't show every extreme that they name: `ancestors`: entry 0 of supernode k's list is its parent, between k + 1 and 8 (8 names the device's separator supernode); entry 1 is a top supernode, 0 to 3. `block_rows`: distinct and increasing within each block. `chain_rows`: distinct and increasing within each block.
All inputs are finite; a program needn't handle non-finite values.
Results may differ from the reference program's by a relative error of at most 0.0003.
Values sent between devices are 32-bit elements; how exact they have to be, the bound alone decides.
A program may use at most 192 MiB of HBM per device.

```python
import jax
import jax.numpy as jnp
from jax import lax

W = 256
R = 256
OFFR = 64
LOC = 8
TOP = 4
NODES = 9
N_LEAF = 4
N_COL = 64


def with_diagonal(jitter, diagonal):
    extent = jitter.shape[-1]
    identity_matrix = jnp.eye(extent, dtype=jnp.float32)
    return jitter * (1.0 - identity_matrix) + identity_matrix * diagonal[..., None]


def pick_rows(key, total_count, extent, picked):
    subkeys = jax.random.split(key, total_count)
    chosen = jax.vmap(lambda subkey: jnp.sort(jax.random.permutation(subkey, extent)[:picked]))(subkeys)
    return chosen.astype(jnp.int32)


def draw_node_inverse(key, part):
    key = jax.random.fold_in(key, 11)
    key_diag, key_off = jax.random.split(key)
    layout = (N_LEAF, N_COL, NODES, W, W)
    jitter = jax.random.normal(key_off, layout, jnp.float32)
    diagonal = jax.random.uniform(key_diag, layout[:-1], jnp.float32, 0.85, 1.15)
    return with_diagonal(jitter * (0.25 / W ** 0.5), diagonal)


def draw_top_inverse(key, part):
    key = jax.random.fold_in(key, 13)
    key_diag, key_off = jax.random.split(key)
    layout = (TOP, W, W)
    jitter = jax.random.normal(key_off, layout, jnp.float32)
    diagonal = jax.random.uniform(key_diag, layout[:-1], jnp.float32, 0.85, 1.15)
    return with_diagonal(jitter * (0.25 / W ** 0.5), diagonal)


def chain_rates(key, share, keep_low, keep_high, inflow):
    key_sluggish_draw, key_retain_draw, key_quick_draw, key_spike_draw, key_cutoff_draw = jax.random.split(key, 5)
    slow_mask = jax.random.uniform(key_sluggish_draw, (N_LEAF, 1, W), jnp.float32) < share
    keep = jax.random.uniform(key_retain_draw, (N_LEAF, 1, W), jnp.float32, keep_low, keep_high)
    slow_rate = jnp.sqrt(jnp.exp(jnp.log(keep) * (2.0 / N_COL)) - inflow)
    fast_rate = jax.random.uniform(key_quick_draw, (N_LEAF, N_COL, W), jnp.float32, 0.3, 0.7)
    spike_factor = jax.random.uniform(key_spike_draw, (N_LEAF, N_COL, 1), jnp.float32) < 2.0 / N_COL
    cutoff_level = jax.random.uniform(key_cutoff_draw, (N_LEAF, N_COL, 1), jnp.float32, 0.55, 0.8)
    speed_rates = jnp.where(slow_mask, slow_rate, fast_rate)
    return speed_rates * jnp.where(spike_factor, cutoff_level, 1.0)


def draw_chain_next(key, part):
    key = jax.random.fold_in(key, 23)
    key_rate, key_off = jax.random.split(key)
    layout = (N_LEAF, N_COL, W, W)
    speed_rates = chain_rates(key_rate, 0.5, 0.3, 0.6, 0.045)
    jitter = jax.random.normal(key_off, layout, jnp.float32)
    return with_diagonal(jitter * (0.05 / W ** 0.5), -speed_rates)


def draw_ancestors(key, part):
    key = jax.random.fold_in(key, 31)
    key_up, key_top = jax.random.split(key)
    minimum_parent = jnp.arange(1, LOC + 1, dtype=jnp.int32)
    parent = jax.random.randint(key_up, (N_LEAF, N_COL, LOC), minimum_parent, LOC + 1, dtype=jnp.int32)
    top_node = jax.random.randint(key_top, (N_LEAF, N_COL, LOC), 0, TOP, dtype=jnp.int32)
    top_node = top_node.at[0, 0, 0].set(TOP - 1)
    top_node = top_node.at[N_LEAF - 1, N_COL - 1, LOC - 1].set(0)
    return jnp.stack([parent, top_node], axis=-1)


def draw_block_rows(key, part):
    key = jax.random.fold_in(key, 41)
    chosen = pick_rows(key, N_LEAF * N_COL * LOC * 2, W, OFFR)
    return chosen.reshape(N_LEAF, N_COL, LOC, 2, OFFR)


def draw_chain_rows(key, part):
    key = jax.random.fold_in(key, 43)
    chosen = pick_rows(key, N_LEAF * N_COL, W, OFFR)
    return chosen.reshape(N_LEAF, N_COL, OFFR)


def plant(entries, stream_key, low, high):
    shape = entries.shape
    place = [jax.random.randint(jax.random.fold_in(stream_key, axis), (), 0, shape[axis]) for axis in range(len(shape))]
    entries = entries.at[tuple(place)].set(low)
    longest = shape.index(max(shape))
    place[longest] = (place[longest] + 1) % shape[longest]
    return entries.at[tuple(place)].set(high)


def level_of(rng, shape, cuts, low, top_value):
    def one(dim, parts):
        draws = jax.random.uniform(jax.random.fold_in(jax.random.fold_in(rng, 6), dim), (parts,), jnp.float32, low / len(cuts), top_value / len(cuts))
        return jnp.repeat(jnp.exp(draws), shape[dim] // parts).reshape((-1,) + (1,) * (len(shape) - dim - 1))

    loudness = one(*cuts[0])
    for cut in cuts[1:]:
        loudness = loudness * one(*cut)
    return loudness


def scatter_about(rng, shape, width, reach, shards=(), kind=jnp.bfloat16):
    values = jax.random.normal(rng, shape, jnp.float32) * width
    if len(shards) > 0:
        values = level_of(rng, shape, shards, -0.22, 0.18) * values
    return jnp.clip(values, min=-reach, max=reach).astype(kind)


def setup_inputs(seed: int = 0) -> dict:
    arg_keys = jax.random.split(jax.random.key(seed), 13)
    return {
        "node_rhs": scatter_about(arg_keys[0], (N_LEAF, N_COL, NODES, W, R), 0.02, 0.125, ((0, 4), (1, 64)), jnp.float32),
        "node_inverse": draw_node_inverse(jax.random.fold_in(arg_keys[12], 71), 0),
        "local_blocks": scatter_about(arg_keys[2], (N_LEAF, N_COL, LOC, 2, OFFR, W), (16 * W) ** -0.5, 0.09375, ((0, 4), (1, 64)), jnp.float32),
        "chain_next": draw_chain_next(jax.random.fold_in(arg_keys[12], 71), 0),
        "chain_top": scatter_about(arg_keys[4], (N_LEAF, N_COL, OFFR, W), (16 * W) ** -0.5, 0.09375, ((0, 4), (1, 64)), jnp.float32),
        "top_rhs": scatter_about(arg_keys[5], (TOP, W, R), 1.0, 6.0, (), jnp.float32),
        "top_inverse": draw_top_inverse(jax.random.fold_in(arg_keys[12], 71), 0),
        "top_next": scatter_about(arg_keys[7], (TOP - 1, W, W), (4 * W) ** -0.5, 0.1875, (), jnp.float32),
        "ancestors": draw_ancestors(jax.random.fold_in(arg_keys[12], 71), 0),
        "block_rows": draw_block_rows(jax.random.fold_in(arg_keys[12], 71), 0),
        "chain_target": plant(jax.random.randint(arg_keys[10], (N_LEAF, N_COL), 0, TOP), jax.random.fold_in(arg_keys[10], 1), 0, TOP - 1).astype(jnp.int32),
        "chain_rows": draw_chain_rows(jax.random.fold_in(arg_keys[12], 71), 0),
    }


precise = lax.Precision.HIGHEST


def product(left, right):
    return jnp.dot(left, right, precision=precise, preferred_element_type=jnp.float32)


def transposed(left, right):
    return lax.dot_general(left, right, (((0,), (0,)), ((), ())), precision=precise, preferred_element_type=jnp.float32)


def local_forward(source, inverse, blocks, links, row_index, top_count):
    node_count = source.shape[0]
    local_count = node_count - 1
    pending = jnp.zeros(source.shape, source.dtype)
    upward = jnp.zeros((top_count,) + source.shape[1:], source.dtype)
    solved = []
    for member in range(local_count):
        result = product(inverse[member], source[member] - pending[member])
        solved.append(result)
        pending = pending.at[links[member, 0], row_index[member, 0]].add(product(blocks[member, 0], result))
        upward = upward.at[links[member, 1], row_index[member, 1]].add(product(blocks[member, 1], result))
    return jnp.stack(solved), source[local_count] - pending[local_count], upward


def local_backward(solved, chain_value, inverse, blocks, links, row_index, top_values):
    local_count = solved.shape[0]
    known_values = jnp.concatenate([jnp.zeros_like(solved), chain_value[None]], axis=0)
    for member in reversed(range(local_count)):
        above_rows = known_values[links[member, 0], row_index[member, 0]]
        beyond = top_values[links[member, 1], row_index[member, 1]]
        result = solved[member] - transposed(blocks[member, 0], above_rows) - transposed(blocks[member, 1], beyond)
        known_values = known_values.at[member].set(transposed(inverse[member], result))
    return known_values


def top_solve(source, inverse, coupling):
    top_count = source.shape[0]
    forward = []
    for member in range(top_count):
        result = source[member]
        if member > 0:
            result = result - product(coupling[member - 1], forward[-1])
        forward.append(product(inverse[member], result))
    backward = [None] * top_count
    for member in reversed(range(top_count)):
        result = forward[member]
        if member < top_count - 1:
            result = result - transposed(coupling[member], backward[member + 1])
        backward[member] = transposed(inverse[member], result)
    return jnp.stack(backward)


def reference(node_rhs, node_inverse, local_blocks, chain_next, chain_top, top_rhs, top_inverse, top_next, ancestors, block_rows, chain_target, chain_rows):
    groups, columns, node_count = node_rhs.shape[0], node_rhs.shape[1], node_rhs.shape[2]
    total_count = groups * columns

    def flatten(array):
        return array.reshape((total_count,) + array.shape[2:])

    def forward_one(pieces):
        source, inverse, blocks, links, row_index = pieces
        return local_forward(source, inverse, blocks, links, row_index, TOP)

    solved, residual, upward = lax.map(forward_one, (flatten(node_rhs), flatten(node_inverse), flatten(local_blocks), flatten(ancestors), flatten(block_rows)))
    residual = residual.reshape(groups, columns, W, R)
    last_column = (jnp.arange(columns) == columns - 1)[None, :, None, None]
    onward = jnp.where(last_column, jnp.zeros_like(chain_next), chain_next)
    chain_inverse = node_inverse[:, :, node_count - 1]
    anchor = jnp.zeros((W, R), node_rhs.dtype)

    def chain_step(carried, pieces):
        lowered, inverse, coupling = pieces
        result = product(inverse, lowered - carried)
        return product(coupling, result), result

    def chain_group(lowered, inverse, coupling):
        return lax.scan(chain_step, anchor, (lowered, inverse, coupling))[1]

    chain_values = jax.vmap(chain_group)(residual, chain_inverse, onward)

    def add_chain(pieces):
        upper, sideways, chain_value, target, row_here = pieces
        return upper.at[target, row_here].add(product(sideways, chain_value))

    targets = chain_target.reshape(total_count)
    upward = lax.map(add_chain, (upward, flatten(chain_top), flatten(chain_values), targets, flatten(chain_rows)))
    top_values = top_solve(top_rhs - jnp.sum(upward, axis=0), top_inverse, top_next)

    def lower_one(pieces):
        chain_value, sideways, target, row_here = pieces
        return chain_value - transposed(sideways, top_values[target, row_here])

    lowered = lax.map(lower_one, (flatten(chain_values), flatten(chain_top), targets, flatten(chain_rows))).reshape(groups, columns, W, R)

    def back_step(carried, pieces):
        lowered_here, inverse, coupling = pieces
        result = transposed(inverse, lowered_here - transposed(coupling, carried))
        return result, result

    def back_group(lowered_here, inverse, coupling):
        return lax.scan(back_step, anchor, (lowered_here, inverse, coupling), reverse=True)[1]

    chain_solution = jax.vmap(back_group)(lowered, chain_inverse, onward)

    def backward_one(pieces):
        solved_here, chain_value, inverse, blocks, links, row_index = pieces
        return local_backward(solved_here, chain_value, inverse, blocks, links, row_index, top_values)

    node_solution = lax.map(backward_one, (solved, flatten(chain_solution), flatten(node_inverse), flatten(local_blocks), flatten(ancestors), flatten(block_rows)))
    return node_solution.reshape(node_rhs.shape), top_values
```

```python
import jax
import jax.numpy as jnp
from jax import lax
from jax.experimental import pallas as pl
from jax.experimental.pallas import tpu as pltpu
from jax.sharding import PartitionSpec as P

F32 = jnp.float32
BF16 = jnp.bfloat16
MESH = pl.DeviceIdType.MESH
NX, NZ, NY, NCOL = 4, 8, 4, 64
W = 256
H = 128
Q = 16
LOC = 8
TOP = 4


def split(value):
    if isinstance(value, tuple):
        return value
    high = value.astype(BF16)
    return high, (value - high.astype(F32)).astype(BF16)


def once(left, right, dims):
    return lax.dot_general(left, right, (dims, ((), ())), preferred_element_type=F32)


def thrice(left, right, dims):
    lh, ll = split(left)
    rh, rl = split(right)
    return once(lh, rh, dims) + (once(lh, rl, dims) + once(ll, rh, dims))


def nn(left, right):
    return thrice(left, right, ((1,), (0,)))


def nt(left, right):
    return thrice(left, right, ((1,), (1,)))


def tn(left, right):
    return thrice(left, right, ((0,), (0,)))


def one_hot(index_row, extent):
    place = lax.broadcasted_iota(jnp.int32, (extent, index_row.shape[1]), 0)
    return jnp.where(place == index_row, 1.0, 0.0).astype(BF16)


def kernel(
    links, target, rhs, inverse, blocks, onward, sideways, top_rhs, top_inverse, top_next, rows, chain_rows,
    out, top_out,
    src, dh, dl, ddh, ddl, hval, upn, upt, uprecv, uph, ybuf, uy, zred,
    a_own, a_sib, a0, a1, msel, nfull, acf, ach, acl, fh, fl, gh, gl, vbuf, pall,
    rt, ex_s, ex_r, schip, sbuf, z0, zsend, zbuf, zback, xin_f, xout_f,
    ar_a, ar_b, ar_c, ar_d, topx, topt, trt, tih, til, kh, kl, lh, ll,
    bt, m_s, m_r, bchip, bbuf, xsend, xback, xin_b, xout_b, mb_s, mb_r,
    core_s, core_r, ac_s, ac_r, acx_s, acx_r, v_s, v_r, vx_s, vx_r, vo_s, vo_r,
    s_s, s_r, up_s, up_r, y_s, y_r, zr_s, zr_r, xf_s, xf_r, zb_s, zb_r, ar_s, ar_r,
    b_s, b_r, xb_s, xb_r, xa_s, xa_r, tp_s, tp_r,
):
    leaf = lax.axis_index("leaf")
    col = lax.axis_index("col")
    x, z, q = col // 16, (col // 2) % NZ, col % 2

    def at(xx, zz, qq):
        return (leaf, xx * 16 + zz * 2 + qq)

    sibling = at(x, z, 1 - q)

    def zpeer(d):
        return at(x, lax.rem(z + d, NZ), q)

    def xpeer(d):
        return at(lax.rem(x + d, NX), z, q)

    def ypeer(d):
        return (lax.rem(leaf + d, NY), col)

    def zfrom(d):
        return lax.rem(z + NZ - d, NZ)

    def xfrom(d):
        return lax.rem(x + NX - d, NX)

    def yfrom(d):
        return lax.rem(leaf + NY - d, NY)

    def copy(source, goal, ss, rs, device):
        return pltpu.make_async_remote_copy(
            src_ref=source, dst_ref=goal, send_sem=ss, recv_sem=rs, device_id=device, device_id_type=MESH
        )

    def swap(source, goal, number):
        return copy(source, goal, core_s.at[number], core_r.at[number], sibling)

    barrier = pltpu.get_barrier_semaphore()
    peers = [sibling] + [zpeer(d) for d in range(1, NZ)] + [xpeer(d) for d in range(1, NX)]
    peers = peers + [ypeer(d) for d in range(1, NY)]
    for peer in peers:
        pl.semaphore_signal(barrier, inc=1, device_id=peer, device_id_type=MESH)

    first = q == 0
    half = pl.ds(pl.multiple_of(q * H, H), H)
    other = pl.ds(pl.multiple_of((1 - q) * H, H), H)

    def rows_of(zz):
        return pl.ds(pl.multiple_of(zz * Q, Q), Q)

    chain_inverse = split(inverse[LOC])
    coupling = jnp.where(col == NCOL - 1, jnp.zeros((W, W), F32), onward[...])
    a_own[...] = -nn(coupling, chain_inverse)
    side = nn(sideways[...], chain_inverse)
    side_h, side_l = split(side)
    spread = one_hot(chain_rows[...], W)
    nfull[...] = once(spread, side_h, ((1,), (0,))) + once(spread, side_l, ((1,), (0,)))

    pl.semaphore_wait(barrier, len(peers))
    swap_a = swap(a_own, a_sib, 0)
    swap_a.start()

    def local_map(k, carry):
        near = nn(blocks[k], inverse[k])
        near_h, near_l = split(near)
        to_parent = one_hot(rows[pl.ds(2 * k, 1), :], W)
        to_top = one_hot(rows[pl.ds(2 * k + 1, 1), :], W)
        dh[k] = once(to_parent, near_h[:64], ((1,), (0,))).astype(BF16)
        dl[k] = once(to_parent, near_l[:64], ((1,), (0,))).astype(BF16)
        ddh[k] = once(to_top, near_h[64:], ((1,), (0,))).astype(BF16)
        ddl[k] = once(to_top, near_l[64:], ((1,), (0,))).astype(BF16)
        return carry

    lax.fori_loop(0, LOC, local_map, 0)

    swap_a.wait()
    a0[...] = jnp.where(first, a_own[...], a_sib[...])
    a1[...] = jnp.where(first, a_sib[...], a_own[...])
    pair = nn(a1[...], a0[...])
    msel[...] = jnp.where(first, pair, a_own[...])
    acf[z] = pair.T
    vbuf[z, q, pl.ds(0, 64)] = jnp.where(first, side, nn(side, a0[...]))
    index = (chain_rows[...] + target[0] * W).astype(F32)
    empty = jnp.zeros((1, 64), F32)
    index = jnp.concatenate(
        [jnp.where(first, index, empty), jnp.where(first, empty, index), jnp.zeros((1, 128), F32)], axis=1
    )
    vbuf[z, q, pl.ds(64, 8)] = jnp.broadcast_to(index, (8, W))

    def ac_copy(d):
        return copy(acf.at[z, half], acf.at[z, half], ac_s.at[d], ac_r.at[d], zpeer(d))

    def v_copy(d):
        return copy(vbuf.at[z, q], vbuf.at[z, q], v_s.at[d], v_r.at[d], zpeer(d))

    order = (1, 7, 2, 6, 3, 5, 4)
    for d in order:
        ac_copy(d).start()
    v_own = copy(vbuf.at[z, q], vbuf.at[z, q], vo_s.at[0], vo_r.at[0], sibling)
    v_own.start()
    for d in order:
        v_copy(d).start()

    for k in range(LOC + 1):
        src[k] = rhs[k]
    for k in range(LOC):
        update = nn((dh[k], dl[k]), src[k])
        for j in range(k + 1, LOC + 1):
            src[j] = src[j] - jnp.where(links[k, 0] == j, update, 0.0)

    rt[...] = src[LOC].T
    ex_s[...] = jnp.where(first, -nt(rt[...], a_own[...]), rt[...])
    swap_s = swap(ex_s, ex_r, 1)
    swap_s.start()
    swap_s.wait()
    shift_half = jnp.where(first, ex_s[half], ex_r[half])
    rest_half = jnp.where(first, ex_r[half], ex_s[half])
    schip[...] = -nt(rest_half - shift_half, a1[...])

    def s_copy(d):
        to = lax.rem(z + d, NZ)
        return copy(schip.at[rows_of(to)], sbuf.at[z], s_s.at[d], s_r.at[d], zpeer(d))

    for d in order:
        s_copy(d).start()
    sbuf[z] = schip[rows_of(z)]

    for t in range(TOP):
        upn[t] = jnp.zeros((W, W), F32)

    def local_up(k, carry):
        part = nn((ddh[k], ddl[k]), src[k])
        for t in range(TOP):
            upn[t] = upn[t] + jnp.where(links[k, 1] == t, part, 0.0)
        return carry

    lax.fori_loop(0, LOC, local_up, 0)
    chain_part = nt(jnp.where(first, rt[...], rt[...] - ex_r[...]), nfull[...])
    for t in range(TOP):
        upt[t] = upn[t].T + jnp.where(target[0] == t, chain_part, 0.0)
    swap_u = copy(upt.at[:, other], uprecv, up_s.at[0], up_r.at[0], sibling)
    swap_u.start()

    def square(k, carry):
        here = split(inverse[k])
        hval[k] = tn(here, nn(here, src[k]))
        return carry

    lax.fori_loop(0, LOC // 2, square, 0)
    swap_u.wait()
    for t in range(TOP):
        uph[t] = upt[t, half] + uprecv[t]

    def y_copy(d):
        return copy(uph.at[lax.rem(leaf + d, NY)], ybuf.at[leaf], y_s.at[d], y_r.at[d], ypeer(d))

    for d in range(1, NY):
        y_copy(d).start()
    ybuf[leaf] = uph[leaf]
    lax.fori_loop(LOC // 2, LOC, square, 0)

    for t in range(TOP):
        th, tl = split(top_inverse[t])
        tih[t] = th
        til[t] = tl
        trt[t] = top_rhs[t].T
    for t in range(TOP - 1):
        kh[t], kl[t] = split(nn((tih[t + 1], til[t + 1]), top_next[t]))
        lh[t], ll[t] = split(nn(top_next[t], (tih[t], til[t])))

    def ac_pass(d):
        part = acf.at[zfrom(d), half]
        return copy(part, part, acx_s.at[d], acx_r.at[d], sibling)

    def ac_come(d):
        part = acf.at[zfrom(d), half]
        return copy(part, part, ac_s.at[d], ac_r.at[d], zpeer(d))

    def ac_passed(d):
        part = acf.at[zfrom(d), other]
        return copy(part, part, acx_s.at[d], acx_r.at[d], sibling)

    def v_come(d):
        part = vbuf.at[zfrom(d), q]
        return copy(part, part, v_s.at[d], v_r.at[d], zpeer(d))

    def v_pass(d):
        part = vbuf.at[zfrom(d), q]
        return copy(part, part, vx_s.at[d], vx_r.at[d], sibling)

    def v_passed(d):
        part = vbuf.at[zfrom(d), 1 - q]
        return copy(part, part, vx_s.at[d], vx_r.at[d], sibling)

    for d in order:
        ac_come(d).wait_recv()
        ac_pass(d).start()
    for d in range(1, NY):
        copy(uph.at[0], ybuf.at[yfrom(d)], y_s.at[d], y_r.at[d], ypeer(d)).wait_recv()
    uy[...] = (ybuf[0] + ybuf[1]) + (ybuf[2] + ybuf[3])

    def zr_copy(d):
        to = lax.rem(z + d, NZ)
        return copy(uy.at[rows_of(to)], zred.at[z], zr_s.at[d], zr_r.at[d], zpeer(d))

    for d in order:
        zr_copy(d).start()
    zred[z] = uy[rows_of(z)]
    for d in order:
        ac_passed(d).wait_recv()

    def halves(c, carry):
        ach[c], acl[c] = split(acf[c])
        return carry

    lax.fori_loop(0, NZ, halves, 0)
    for d in order:
        copy(schip.at[pl.ds(0, Q)], sbuf.at[zfrom(d)], s_s.at[d], s_r.at[d], zpeer(d)).wait_recv()

    z0[0] = sbuf[0]
    fh[0] = ach[0]
    fl[0] = acl[0]

    def prefix(c, carry):
        here = (ach[c], acl[c])
        z0[c] = sbuf[c] + nn(z0[c - 1], here)
        fh[c], fl[c] = split(nn((fh[c - 1], fl[c - 1]), here))
        return carry

    lax.fori_loop(1, NZ, prefix, 0)

    whole = (fh[NZ - 1], fl[NZ - 1])
    hop_f = copy(xout_f, xin_f, xf_s.at[0], xf_r.at[0], at(lax.rem(x + 1, NX), z, q))

    @pl.when(x == 0)
    def _():
        xin_f[...] = jnp.zeros((Q, W), F32)
        xout_f[...] = z0[NZ - 1]

    @pl.when(x > 0)
    def _():
        hop_f.wait_recv()
        xout_f[...] = z0[NZ - 1] + nn(xin_f[...], whole)

    @pl.when(x < NX - 1)
    def _():
        hop_f.start()

    entering = split(xin_f[...])
    zsend[0] = xin_f[...]

    def fix(c, carry):
        zsend[c] = z0[c - 1] + nn(entering, (fh[c - 1], fl[c - 1]))
        return carry

    lax.fori_loop(1, NZ, fix, 0)

    def zb_copy(d):
        to = lax.rem(z + d, NZ)
        return copy(zsend.at[to], zback.at[rows_of(z)], zb_s.at[d], zb_r.at[d], zpeer(d))

    for d in order:
        zb_copy(d).start()
    zback[rows_of(z)] = zsend[z]

    for d in order:
        v_come(d).wait_recv()
        v_pass(d).start()
    v_own_come = copy(vbuf.at[z, 1 - q], vbuf.at[z, 1 - q], vo_s.at[0], vo_r.at[0], sibling)
    v_own_come.wait_recv()
    for d in order:
        v_passed(d).wait_recv()

    flows = []
    for c in range(NZ):
        found = (vbuf[c, 0, pl.ds(64, 1), pl.ds(0, H)] + vbuf[c, 1, pl.ds(64, 1), pl.ds(0, H)]).astype(jnp.int32)
        pall[:, c * H : (c + 1) * H] = one_hot(found, TOP * W)
        reach = jnp.concatenate([vbuf[c, 0, pl.ds(0, 64)], vbuf[c, 1, pl.ds(0, 64)]], axis=0)
        flows.append(nt(zsend[c], reach))
    flow_h, flow_l = split(jnp.concatenate(flows, axis=1))
    for d in order:
        copy(uy.at[pl.ds(0, Q)], zred.at[zfrom(d)], zr_s.at[d], zr_r.at[d], zpeer(d)).wait_recv()
    reduced = zred[0]
    for c in range(1, NZ):
        reduced = reduced + zred[c]
    for t in range(TOP):
        places = pall[t * W : (t + 1) * W, :]
        down = once(flow_h, places, ((1,), (1,))) + once(flow_l, places, ((1,), (1,)))
        part = jnp.where(leaf == t, reduced, 0.0) - down
        if t < 2:
            ar_a[x, t] = part
        else:
            ar_b[leaf, t - 2] = part

    def ar_copy(buf, mine, number, device):
        return copy(buf.at[mine], buf.at[mine], ar_s.at[number], ar_r.at[number], device)

    for d in range(1, NX):
        ar_copy(ar_a, x, d, xpeer(d)).start()
        ar_copy(ar_b, leaf, 4 + d, ypeer(d)).start()

    gh[NZ - 1] = ach[NZ - 1]
    gl[NZ - 1] = acl[NZ - 1]

    def suffix(i, carry):
        c = NZ - 1 - i
        gh[c], gl[c] = split(nn((ach[c], acl[c]), (gh[c + 1], gl[c + 1])))
        return carry

    lax.fori_loop(1, NZ, suffix, 0)

    for d in order:
        copy(zsend.at[0], zback.at[rows_of(zfrom(d))], zb_s.at[d], zb_r.at[d], zpeer(d)).wait_recv()
    swap_z = swap(zback, zbuf, 2)
    swap_z.start()

    for d in range(1, NX):
        ar_copy(ar_a, xfrom(d), d, xpeer(d)).wait_recv()
        ar_copy(ar_b, yfrom(d), 4 + d, ypeer(d)).wait_recv()
    ar_c[leaf] = (ar_a[0] + ar_a[1]) + (ar_a[2] + ar_a[3])
    ar_d[x] = (ar_b[0] + ar_b[1]) + (ar_b[2] + ar_b[3])
    for d in range(1, NX):
        ar_copy(ar_c, leaf, 8 + d, ypeer(d)).start()
        ar_copy(ar_d, x, 12 + d, xpeer(d)).start()

    swap_z.wait()
    mine, theirs = zback[...], zbuf[...]
    entry = jnp.concatenate([jnp.where(first, mine, theirs), jnp.where(first, theirs, mine)], axis=0)
    inner = ex_r[...] + nt(entry, a0[...])
    entry = jnp.where(first, entry, inner)
    chain_inverse = split(inverse[LOC])
    bt[...] = nn(nt(rt[...] - entry, chain_inverse), chain_inverse)
    m_s[...] = jnp.where(first, bt[...], nn(bt[...], a0[...]))
    swap_m = swap(m_s, m_r, 3)
    swap_m.start()
    swap_m.wait()
    bchip[...] = m_s[half] + m_r[half]

    def b_copy(d):
        to = lax.rem(z + d, NZ)
        return copy(bchip.at[rows_of(to)], bbuf.at[z], b_s.at[d], b_r.at[d], zpeer(d))

    for d in order:
        b_copy(d).start()
    bbuf[z] = bchip[rows_of(z)]

    for d in range(1, NX):
        ar_copy(ar_c, yfrom(d), 8 + d, ypeer(d)).wait_recv()
        ar_copy(ar_d, xfrom(d), 12 + d, xpeer(d)).wait_recv()
    low = (ar_c[0] + ar_c[1]) + (ar_c[2] + ar_c[3])
    high = (ar_d[0] + ar_d[1]) + (ar_d[2] + ar_d[3])
    mine_rows = pl.ds(pl.multiple_of(q * H + z * Q, Q), Q)

    sums = [low[0], low[1], high[0], high[1]]
    forward = []
    for t in range(TOP):
        value = nt(trt[t, mine_rows] - sums[t], (tih[t], til[t]))
        if t > 0:
            value = value - nt(forward[-1], (kh[t - 1], kl[t - 1]))
        forward.append(value)
    above = None
    found = [None] * TOP
    for t in reversed(range(TOP)):
        value = nn(forward[t], (tih[t], til[t]))
        if t < TOP - 1:
            value = value - nn(above, (lh[t], ll[t]))
        above = value
        found[t] = value
        topx[t] = value

    def tp_copy(d):
        return copy(topx, topt.at[:, mine_rows], tp_s.at[d], tp_r.at[d], zpeer(d))

    for d in order:
        tp_copy(d).start()
    topt[:, mine_rows] = topx[...]

    found_h, found_l = split(jnp.concatenate(found, axis=1))
    picked = once(found_h, pall[...], ((1,), (0,))) + once(found_l, pall[...], ((1,), (0,)))
    for d in order:
        copy(bchip.at[pl.ds(0, Q)], bbuf.at[zfrom(d)], b_s.at[d], b_r.at[d], zpeer(d)).wait_recv()
    for c in range(NZ):
        reach = jnp.concatenate([vbuf[c, 0, pl.ds(0, 64)], vbuf[c, 1, pl.ds(0, 64)]], axis=0)
        z0[c] = bbuf[c] - nn(picked[:, c * H : (c + 1) * H], reach)

    def back(i, carry):
        c = NZ - 1 - i
        z0[c] = z0[c] + nt(z0[c + 1], (ach[c], acl[c]))
        return carry

    lax.fori_loop(1, NZ, back, 0)

    hop_b = copy(xout_b, xin_b, xb_s.at[0], xb_r.at[0], at(lax.rem(x + NX - 1, NX), z, q))

    @pl.when(x == NX - 1)
    def _():
        xin_b[...] = jnp.zeros((Q, W), F32)
        xout_b[...] = z0[0]

    @pl.when(x < NX - 1)
    def _():
        hop_b.wait_recv()
        xout_b[...] = z0[0] + nt(xin_b[...], (fh[NZ - 1], fl[NZ - 1]))

    @pl.when(x > 0)
    def _():
        hop_b.start()

    leaving = split(xin_b[...])
    xsend[NZ - 1] = xin_b[...]

    def unfix(c, carry):
        xsend[c] = z0[c + 1] + nt(leaving, (gh[c + 1], gl[c + 1]))
        return carry

    lax.fori_loop(0, NZ - 1, unfix, 0)

    def xa_copy(d):
        to = lax.rem(z + d, NZ)
        return copy(xsend.at[to], xback.at[rows_of(z)], xa_s.at[d], xa_r.at[d], zpeer(d))

    for d in order:
        xa_copy(d).start()
    xback[rows_of(z)] = xsend[z]

    for d in order:
        place = pl.ds(pl.multiple_of(q * H + zfrom(d) * Q, Q), Q)
        copy(topx, topt.at[:, place], tp_s.at[d], tp_r.at[d], zpeer(d)).wait_recv()
    swap_t = copy(topt.at[:, half], topt.at[:, half], up_s.at[1], up_r.at[1], sibling)
    swap_t.start()
    swap_t.wait_send()
    copy(topt.at[:, other], topt.at[:, other], up_s.at[1], up_r.at[1], sibling).wait_recv()
    bt[...] = bt[...] - nn(topt[target[0]], nfull[...])
    mb_s[...] = nn(bt[...], a0[...])
    swap_b = swap(mb_s, mb_r, 4)
    swap_b.start()
    for t in range(TOP):
        top_out[t] = topt[t].T

    def lower(k, carry):
        hval[k] = hval[k] - tn((ddh[k], ddl[k]), top_out[links[k, 1]])
        return carry

    lax.fori_loop(0, LOC, lower, 0)
    swap_b.wait()
    base = bt[...] + jnp.where(first, mb_r[...], 0.0)

    for d in order:
        copy(xsend.at[0], xback.at[rows_of(zfrom(d))], xa_s.at[d], xa_r.at[d], zpeer(d)).wait_recv()
    swap_x = swap(xback, zbuf, 5)
    swap_x.start()
    swap_x.wait()
    mine, theirs = xback[...], zbuf[...]
    exits = jnp.concatenate([jnp.where(first, mine, theirs), jnp.where(first, theirs, mine)], axis=0)
    out[LOC] = (base + nn(exits, msel[...])).T

    def local_back(i, carry):
        k = LOC - 1 - i
        out[k] = hval[k] - tn((dh[k], dl[k]), out[links[k, 0]])
        return carry

    lax.fori_loop(0, LOC, local_back, 0)

    for d in order:
        ac_copy(d).wait_send()
        v_copy(d).wait_send()
        ac_pass(d).wait_send()
        v_pass(d).wait_send()
        s_copy(d).wait_send()
        zr_copy(d).wait_send()
        zb_copy(d).wait_send()
        b_copy(d).wait_send()
        tp_copy(d).wait_send()
        xa_copy(d).wait_send()
    v_own.wait_send()
    for d in range(1, NX):
        y_copy(d).wait_send()
        ar_copy(ar_a, x, d, xpeer(d)).wait_send()
        ar_copy(ar_b, leaf, 4 + d, ypeer(d)).wait_send()
        ar_copy(ar_c, leaf, 8 + d, ypeer(d)).wait_send()
        ar_copy(ar_d, x, 12 + d, xpeer(d)).wait_send()

    @pl.when(x < NX - 1)
    def _():
        hop_f.wait_send()

    @pl.when(x > 0)
    def _():
        hop_b.wait_send()


def shards(
    node_rhs, node_inverse, local_blocks, chain_next, chain_top, top_rhs, top_inverse, top_next,
    ancestors, block_rows, chain_target, chain_rows,
):
    vmem = pl.BlockSpec(memory_space=pltpu.VMEM)
    smem = pl.BlockSpec(memory_space=pltpu.SMEM)

    def f32(*shape):
        return pltpu.VMEM(shape, F32)

    def b16(*shape):
        return pltpu.VMEM(shape, BF16)

    def sem(count):
        return pltpu.SemaphoreType.DMA((count,))

    scratch = [
        f32(LOC + 1, W, W), b16(LOC, W, W), b16(LOC, W, W), b16(LOC, W, W), b16(LOC, W, W), f32(LOC, W, W),
        f32(TOP, W, W), f32(TOP, W, W), f32(TOP, H, W), f32(TOP, H, W), f32(NY, H, W), f32(H, W), f32(NZ, Q, W),
        f32(W, W), f32(W, W), f32(W, W), f32(W, W), f32(W, W), f32(W, W),
        f32(NZ, W, W), b16(NZ, W, W), b16(NZ, W, W), b16(NZ, W, W), b16(NZ, W, W), b16(NZ, W, W), b16(NZ, W, W),
        f32(NZ, 2, 72, W), b16(TOP * W, NZ * H),
        f32(W, W), f32(W, W), f32(W, W), f32(H, W), f32(NZ, Q, W), f32(NZ, Q, W), f32(NZ, Q, W), f32(H, W),
        f32(H, W), f32(Q, W), f32(Q, W),
        f32(NX, 2, Q, W), f32(NY, 2, Q, W), f32(NY, 2, Q, W), f32(NX, 2, Q, W),
        f32(TOP, Q, W), f32(TOP, W, W), f32(TOP, W, W), b16(TOP, W, W), b16(TOP, W, W),
        b16(TOP - 1, W, W), b16(TOP - 1, W, W), b16(TOP - 1, W, W), b16(TOP - 1, W, W),
        f32(W, W), f32(W, W), f32(W, W), f32(H, W), f32(NZ, Q, W), f32(NZ, Q, W), f32(H, W),
        f32(Q, W), f32(Q, W), f32(W, W), f32(W, W),
        sem(6), sem(6), sem(8), sem(8), sem(8), sem(8), sem(8), sem(8), sem(8), sem(8), sem(1), sem(1),
        sem(8), sem(8), sem(2), sem(2), sem(4), sem(4), sem(8), sem(8), sem(1), sem(1), sem(8), sem(8),
        sem(16), sem(16), sem(8), sem(8), sem(1), sem(1), sem(8), sem(8), sem(8), sem(8),
    ]
    solved, top = pl.pallas_call(
        kernel,
        out_shape=(
            jax.ShapeDtypeStruct((LOC + 1, W, W), F32),
            jax.ShapeDtypeStruct((TOP, W, W), F32),
        ),
        in_specs=[smem, smem] + [vmem] * 10,
        out_specs=(vmem, vmem),
        scratch_shapes=scratch,
        compiler_params=pltpu.CompilerParams(
            collective_id=0, has_side_effects=True, vmem_limit_bytes=56 * 1024 * 1024
        ),
    )(
        ancestors[0, 0],
        chain_target[0],
        node_rhs[0, 0],
        node_inverse[0, 0],
        local_blocks[0, 0].reshape(LOC, 128, W),
        chain_next[0, 0],
        chain_top[0, 0],
        top_rhs,
        top_inverse,
        top_next,
        block_rows[0, 0].reshape(2 * LOC, 64),
        chain_rows[0],
    )
    return solved[None, None], top


def solution(mesh):
    placed = (
        P("leaf", "col", None, None, None),
        P("leaf", "col", None, None, None),
        P("leaf", "col", None, None, None, None),
        P("leaf", "col", None, None),
        P("leaf", "col", None, None),
        P(),
        P(),
        P(),
        P("leaf", "col", None, None),
        P("leaf", "col", None, None, None),
        P("leaf", "col"),
        P("leaf", "col", None),
    )
    return jax.shard_map(
        shards,
        mesh=mesh,
        in_specs=placed,
        out_specs=(P("leaf", "col", None, None, None), P()),
        check_vma=False,
    )
```

```python
import jax
import jax.numpy as jnp
from jax import lax
from jax.experimental import pallas as pl
from jax.experimental.pallas import tpu as pltpu
from jax.sharding import PartitionSpec as P

F32 = jnp.float32
BF16 = jnp.bfloat16
MESH = pl.DeviceIdType.MESH
NX, NZ, NY, NCOL = 4, 8, 4, 64
W = 256
H = 128
Q = 16
LOC = 8
TOP = 4


def split(value):
    if isinstance(value, tuple):
        return value
    high = value.astype(BF16)
    return high, (value - high.astype(F32)).astype(BF16)


def once(left, right, dims):
    return lax.dot_general(left, right, (dims, ((), ())), preferred_element_type=F32)


def thrice(left, right, dims):
    lh, ll = split(left)
    rh, rl = split(right)
    return once(lh, rh, dims) + (once(lh, rl, dims) + once(ll, rh, dims))


def nn(left, right):
    return thrice(left, right, ((1,), (0,)))


def nt(left, right):
    return thrice(left, right, ((1,), (1,)))


def tn(left, right):
    return thrice(left, right, ((0,), (0,)))


def one_hot(index_row, extent):
    place = lax.broadcasted_iota(jnp.int32, (extent, index_row.shape[1]), 0)
    return jnp.where(place == index_row, 1.0, 0.0).astype(BF16)


def kernel(
    links, target, rhs_in, inverse_in, blocks_in, onward, sideways, top_rhs_in, top_inverse_in, top_next_in, rows, chain_rows,
    out_to, top_to,
    src, inverse, blocks, top_rhs, top_inverse, top_next, out, top_out,
    dh, dl, n1h, n1l, ycat, pt, hval, upt, uprecv, uph, ybuf, uy, zred,
    a_own, a_sib, a0, a1, msel, side_v, acf, ach, acl, fh, fl, gh, gl, vbuf, pall,
    rt, ex_s, ex_r, schip, sbuf, z0, zsend, zbuf, zback, xin_f, xout_f,
    ar_a, ar_b, ar_c, ar_d, topx, topt, trt, tih, til, kh, kl, lh, ll,
    bt, m_s, m_r, bchip, bbuf, xsend, xback, xin_b, xout_b, mb_s, mb_r,
    load, store, core_s, core_r, ac_s, ac_r, acx_s, acx_r, v_s, v_r, vx_s, vx_r, vo_s, vo_r,
    s_s, s_r, up_s, up_r, y_s, y_r, zr_s, zr_r, xf_s, xf_r, zb_s, zb_r, ar_s, ar_r,
    b_s, b_r, xb_s, xb_r, xa_s, xa_r, tp_s, tp_r,
):
    leaf = lax.axis_index("leaf")
    col = lax.axis_index("col")
    x, z, q = col // 16, (col // 2) % NZ, col % 2

    def at(xx, zz, qq):
        return (leaf, xx * 16 + zz * 2 + qq)

    sibling = at(x, z, 1 - q)

    def zpeer(d):
        return at(x, lax.rem(z + d, NZ), q)

    def xpeer(d):
        return at(lax.rem(x + d, NX), z, q)

    def ypeer(d):
        return (lax.rem(leaf + d, NY), col)

    def zfrom(d):
        return lax.rem(z + NZ - d, NZ)

    def xfrom(d):
        return lax.rem(x + NX - d, NX)

    def yfrom(d):
        return lax.rem(leaf + NY - d, NY)

    def copy(source, goal, ss, rs, device):
        return pltpu.make_async_remote_copy(
            src_ref=source, dst_ref=goal, send_sem=ss, recv_sem=rs, device_id=device, device_id_type=MESH
        )

    def swap(source, goal, number):
        return copy(source, goal, core_s.at[number], core_r.at[number], sibling)

    barrier = pltpu.get_barrier_semaphore()
    peers = [sibling] + [zpeer(d) for d in range(1, NZ)] + [xpeer(d) for d in range(1, NX)]
    peers = peers + [ypeer(d) for d in range(1, NY)]
    for peer in peers:
        pl.semaphore_signal(barrier, inc=1, device_id=peer, device_id_type=MESH)

    loads = [
        pltpu.make_async_copy(inverse_in.at[LOC], inverse.at[LOC], load.at[0]),
        pltpu.make_async_copy(inverse_in.at[pl.ds(0, LOC)], inverse.at[pl.ds(0, LOC)], load.at[1]),
        pltpu.make_async_copy(blocks_in, blocks, load.at[2]),
        pltpu.make_async_copy(rhs_in, src, load.at[3]),
        pltpu.make_async_copy(top_inverse_in, top_inverse, load.at[4]),
        pltpu.make_async_copy(top_next_in, top_next, load.at[5]),
        pltpu.make_async_copy(top_rhs_in, top_rhs, load.at[6]),
    ]
    for item in loads:
        item.start()

    first = q == 0
    half = pl.ds(pl.multiple_of(q * H, H), H)
    other = pl.ds(pl.multiple_of((1 - q) * H, H), H)

    def rows_of(zz):
        return pl.ds(pl.multiple_of(zz * Q, Q), Q)

    def by_four(body):
        def four(i, carry):
            for j in range(4):
                body(4 * i + j)
            return carry

        lax.fori_loop(0, 2, four, 0)

    loads[0].wait()
    chain_inverse = split(inverse[LOC])
    coupling = jnp.where(col == NCOL - 1, jnp.zeros((W, W), F32), onward[...])
    a_own[...] = -nn(coupling, chain_inverse)
    pl.semaphore_wait(barrier, len(peers))
    swap_a = swap(a_own, a_sib, 0)
    swap_a.start()
    side = nn(sideways[...], chain_inverse)
    side_v[...] = side
    loads[1].wait()
    loads[2].wait()

    def local_map(k):
        near = nn(blocks[k], inverse[k])
        near_h, near_l = split(near)
        to_parent = one_hot(rows[pl.ds(2 * k, 1), :], W)
        dh[k] = once(to_parent, near_h[:64], ((1,), (0,))).astype(BF16)
        dl[k] = once(to_parent, near_l[:64], ((1,), (0,))).astype(BF16)
        n1h[k] = near_h[64:]
        n1l[k] = near_l[64:]

    def some_maps(start):
        def two(i, carry):
            local_map(start + 2 * i)
            local_map(start + 2 * i + 1)
            return carry

        lax.fori_loop(0, 2, two, 0)

    swap_a.wait_recv()
    a0[...] = jnp.where(first, a_own[...], a_sib[...])
    a1[...] = jnp.where(first, a_sib[...], a_own[...])
    pair = nn(a1[...], a0[...])
    acf[z] = pair.T

    def ring_part(core, way, s, h):
        slot = lax.rem(z + NZ - s * way, NZ)
        return acf.at[slot, pl.ds(pl.multiple_of(core * H + h * 64, 64), 64)]

    def ring_number(way, s, h):
        return ((way + 1) // 2 * 4 + s) * 2 + h

    def ring(way, s, h):
        part, i = ring_part(q, way, s, h), ring_number(way, s, h)
        return copy(part, part, ac_s.at[i], ac_r.at[i], zpeer(way % NZ))

    def ring_in(way, s, h):
        part, i = ring_part(q, way, s + 1, h), ring_number(way, s, h)
        return copy(part, part, ac_s.at[i], ac_r.at[i], zpeer(way % NZ))

    def ring_pass(way, s, h):
        part, i = ring_part(q, way, s + 1, h), ring_number(way, s, h)
        return copy(part, part, acx_s.at[i], acx_r.at[i], sibling)

    def ring_passed(way, s, h):
        part, i = ring_part(1 - q, way, s + 1, h), ring_number(way, s, h)
        return copy(part, part, acx_s.at[i], acx_r.at[i], sibling)

    moves = [[(way, s, h) for h in range(2) for way in (1, -1)] for s in range(3)]
    moves.append([(1, 3, 0), (-1, 3, 1)])

    def ring_step(s):
        if s > 0:
            for way, _, h in moves[s - 1]:
                ring_in(way, s - 1, h).wait_recv()
                if s < 4 and (way, s, h) in moves[s]:
                    ring(way, s, h).start()
                ring_pass(way, s - 1, h).start()
        else:
            for way, _, h in moves[0]:
                ring(way, 0, h).start()

    ring_step(0)
    msel[...] = jnp.where(first, pair, a_own[...])
    vbuf[z, q, pl.ds(0, 64)] = jnp.where(first, side, nn(side, a0[...]))
    index = (chain_rows[...] + target[0] * W).astype(F32)
    empty = jnp.zeros((1, 64), F32)
    index = jnp.concatenate(
        [jnp.where(first, index, empty), jnp.where(first, empty, index), jnp.zeros((1, 128), F32)], axis=1
    )
    vbuf[z, q, pl.ds(64, 8)] = jnp.broadcast_to(index, (8, W))

    def v_copy(d):
        return copy(vbuf.at[z, q], vbuf.at[z, q], v_s.at[d], v_r.at[d], zpeer(d))

    order = (1, 7, 2, 6, 3, 5, 4)
    v_own = copy(vbuf.at[z, q], vbuf.at[z, q], vo_s.at[0], vo_r.at[0], sibling)
    v_own.start()
    some_maps(0)
    ring_step(1)
    some_maps(4)
    ring_step(2)
    loads[3].wait()

    for k in range(LOC):
        update = nn((dh[k], dl[k]), src[k])
        for j in range(k + 1, LOC + 1):
            src[j] = src[j] - jnp.where(links[0, k] == j, update, 0.0)
        if k == 2:
            ring_step(3)
        if k == 6:
            ring_step(4)

    rt[...] = src[LOC].T
    ex_s[...] = jnp.where(first, -nt(rt[...], a_own[...]), rt[...])
    swap_s = swap(ex_s, ex_r, 1)
    swap_s.start()
    swap_s.wait_recv()
    shift_half = jnp.where(first, ex_s[half], ex_r[half])
    rest_half = jnp.where(first, ex_r[half], ex_s[half])
    schip[...] = -nt(rest_half - shift_half, a1[...])

    def s_copy(d):
        to = lax.rem(z + d, NZ)
        return copy(schip.at[rows_of(to)], sbuf.at[z], s_s.at[d], s_r.at[d], zpeer(d))

    for d in order:
        s_copy(d).start()
    sbuf[z] = schip[rows_of(z)]

    for d in order:
        v_copy(d).start()

    def up_part(k):
        ycat[pl.ds(pl.multiple_of(k * 64, 64), 64)] = nn((n1h[k], n1l[k]), src[k])

    by_four(up_part)
    diagonal = lax.broadcasted_iota(jnp.int32, (64, 64), 0) == lax.broadcasted_iota(jnp.int32, (64, 64), 1)

    def places_of(index_row):
        column = jnp.sum(jnp.where(diagonal, index_row, 0.0), axis=1, keepdims=True).astype(jnp.int32)
        place = lax.broadcasted_iota(jnp.int32, (64, TOP * W), 1)
        return jnp.where(place == column, 1.0, 0.0).astype(BF16)

    def places_body(k):
        index_row = (rows[pl.ds(2 * k + 1, 1), :] + links[1, k] * W).astype(F32)
        pt[pl.ds(pl.multiple_of(k * 64, 64), 64)] = places_of(index_row)

    by_four(places_body)
    pt[pl.ds(512, 64)] = places_of((chain_rows[...] + target[0] * W).astype(F32))
    up_h, up_l = split(ycat[...].T)
    chain_h, chain_l = split(nt(jnp.where(first, rt[...], rt[...] - ex_r[...]), side_v[...]))
    for t in range(TOP):
        here = pl.ds(t * W, W)
        near, far = pt[pl.ds(0, 512), here], pt[pl.ds(512, 64), here]
        near = once(up_h, near, ((1,), (0,))) + once(up_l, near, ((1,), (0,)))
        far = once(chain_h, far, ((1,), (0,))) + once(chain_l, far, ((1,), (0,)))
        upt[t] = near + far
    swap_u = copy(upt.at[:, other], uprecv, up_s.at[0], up_r.at[0], sibling)
    swap_u.start()

    for item in loads[4:]:
        item.wait()
    for t in range(TOP):
        th, tl = split(top_inverse[t])
        tih[t] = th
        til[t] = tl
        trt[t] = top_rhs[t].T
    for t in range(TOP - 1):
        kh[t], kl[t] = split(nn((tih[t + 1], til[t + 1]), top_next[t]))
        lh[t], ll[t] = split(nn(top_next[t], (tih[t], til[t])))
    swap_u.wait_recv()
    for t in range(TOP):
        uph[t] = upt[t, half] + uprecv[t]

    def y_copy(d):
        return copy(uph.at[lax.rem(leaf + d, NY)], ybuf.at[leaf], y_s.at[d], y_r.at[d], ypeer(d))

    for d in range(1, NY):
        y_copy(d).start()
    ybuf[leaf] = uph[leaf]

    def square(k):
        here = split(inverse[k])
        hval[k] = tn(here, nn(here, src[k]))

    def v_come(d):
        part = vbuf.at[zfrom(d), q]
        return copy(part, part, v_s.at[d], v_r.at[d], zpeer(d))

    def v_pass(d):
        part = vbuf.at[zfrom(d), q]
        return copy(part, part, vx_s.at[d], vx_r.at[d], sibling)

    def v_passed(d):
        part = vbuf.at[zfrom(d), 1 - q]
        return copy(part, part, vx_s.at[d], vx_r.at[d], sibling)

    for step in moves:
        for move in step:
            ring_passed(*move).wait_recv()

    def halves(c, carry):
        ach[c], acl[c] = split(acf[c])
        return carry

    lax.fori_loop(0, NZ, halves, 0)
    for d in order:
        copy(schip.at[pl.ds(0, Q)], sbuf.at[zfrom(d)], s_s.at[d], s_r.at[d], zpeer(d)).wait_recv()

    z0[0] = sbuf[0]
    fh[0] = ach[0]
    fl[0] = acl[0]

    def prefix(c, carry):
        here = (ach[c], acl[c])
        z0[c] = sbuf[c] + nn(z0[c - 1], here)
        fh[c], fl[c] = split(nn((fh[c - 1], fl[c - 1]), here))
        return carry

    lax.fori_loop(1, NZ, prefix, 0)

    @pl.when(x >= 2)
    def _():
        by_four(square)

    whole = (fh[NZ - 1], fl[NZ - 1])
    hop_f = copy(xout_f, xin_f, xf_s.at[0], xf_r.at[0], at(lax.rem(x + 1, NX), z, q))

    @pl.when(x == 0)
    def _():
        xin_f[...] = jnp.zeros((Q, W), F32)
        xout_f[...] = z0[NZ - 1]

    @pl.when(x > 0)
    def _():
        hop_f.wait_recv()
        xout_f[...] = z0[NZ - 1] + nn(xin_f[...], whole)

    @pl.when(x < NX - 1)
    def _():
        hop_f.start()

    for d in range(1, NY):
        copy(uph.at[0], ybuf.at[yfrom(d)], y_s.at[d], y_r.at[d], ypeer(d)).wait_recv()
    uy[...] = (ybuf[0] + ybuf[1]) + (ybuf[2] + ybuf[3])

    def zr_copy(d):
        to = lax.rem(z + d, NZ)
        return copy(uy.at[rows_of(to)], zred.at[z], zr_s.at[d], zr_r.at[d], zpeer(d))

    for d in order:
        zr_copy(d).start()
    zred[z] = uy[rows_of(z)]

    @pl.when(x < 2)
    def _():
        by_four(square)

    entering = split(xin_f[...])
    zsend[0] = xin_f[...]

    def fix(c, carry):
        zsend[c] = z0[c - 1] + nn(entering, (fh[c - 1], fl[c - 1]))
        return carry

    lax.fori_loop(1, NZ, fix, 0)

    def zb_copy(d):
        to = lax.rem(z + d, NZ)
        return copy(zsend.at[to], zback.at[rows_of(z)], zb_s.at[d], zb_r.at[d], zpeer(d))

    for d in order:
        zb_copy(d).start()
    zback[rows_of(z)] = zsend[z]

    for d in order:
        v_come(d).wait_recv()
        v_pass(d).start()
    v_own_come = copy(vbuf.at[z, 1 - q], vbuf.at[z, 1 - q], vo_s.at[0], vo_r.at[0], sibling)
    v_own_come.wait_recv()
    for d in order:
        v_passed(d).wait_recv()

    flows = []
    for c in range(NZ):
        found = (vbuf[c, 0, pl.ds(64, 1), pl.ds(0, H)] + vbuf[c, 1, pl.ds(64, 1), pl.ds(0, H)]).astype(jnp.int32)
        pall[:, c * H : (c + 1) * H] = one_hot(found, TOP * W)
        reach = jnp.concatenate([vbuf[c, 0, pl.ds(0, 64)], vbuf[c, 1, pl.ds(0, 64)]], axis=0)
        flows.append(nt(zsend[c], reach))
    flow_h, flow_l = split(jnp.concatenate(flows, axis=1))
    for d in order:
        copy(uy.at[pl.ds(0, Q)], zred.at[zfrom(d)], zr_s.at[d], zr_r.at[d], zpeer(d)).wait_recv()
    reduced = zred[0]
    for c in range(1, NZ):
        reduced = reduced + zred[c]
    for t in range(TOP):
        places = pall[t * W : (t + 1) * W, :]
        down = once(flow_h, places, ((1,), (1,))) + once(flow_l, places, ((1,), (1,)))
        part = jnp.where(leaf == t, reduced, 0.0) - down
        if t < 2:
            ar_a[x, t] = part
        else:
            ar_b[leaf, t - 2] = part

    def ar_copy(buf, mine, number, device):
        return copy(buf.at[mine], buf.at[mine], ar_s.at[number], ar_r.at[number], device)

    for d in range(1, NX):
        ar_copy(ar_a, x, d, xpeer(d)).start()
        ar_copy(ar_b, leaf, 4 + d, ypeer(d)).start()

    gh[NZ - 1] = ach[NZ - 1]
    gl[NZ - 1] = acl[NZ - 1]

    def suffix(i, carry):
        c = NZ - 1 - i
        gh[c], gl[c] = split(nn((ach[c], acl[c]), (gh[c + 1], gl[c + 1])))
        return carry

    lax.fori_loop(1, NZ, suffix, 0)

    for d in order:
        copy(zsend.at[0], zback.at[rows_of(zfrom(d))], zb_s.at[d], zb_r.at[d], zpeer(d)).wait_recv()
    swap_z = swap(zback, zbuf, 2)
    swap_z.start()

    for d in range(1, NX):
        ar_copy(ar_a, xfrom(d), d, xpeer(d)).wait_recv()
        ar_copy(ar_b, yfrom(d), 4 + d, ypeer(d)).wait_recv()
    ar_c[leaf] = (ar_a[0] + ar_a[1]) + (ar_a[2] + ar_a[3])
    ar_d[x] = (ar_b[0] + ar_b[1]) + (ar_b[2] + ar_b[3])
    for d in range(1, NX):
        ar_copy(ar_c, leaf, 8 + d, ypeer(d)).start()
        ar_copy(ar_d, x, 12 + d, xpeer(d)).start()

    swap_z.wait_recv()
    mine, theirs = zback[...], zbuf[...]
    entry = jnp.concatenate([jnp.where(first, mine, theirs), jnp.where(first, theirs, mine)], axis=0)
    inner = ex_r[...] + nt(entry, a0[...])
    entry = jnp.where(first, entry, inner)
    chain_inverse = split(inverse[LOC])
    bt[...] = nn(nt(rt[...] - entry, chain_inverse), chain_inverse)
    m_s[...] = jnp.where(first, bt[...], nn(bt[...], a0[...]))
    swap_m = swap(m_s, m_r, 3)
    swap_m.start()
    swap_m.wait_recv()
    bchip[...] = m_s[half] + m_r[half]

    def b_copy(d):
        to = lax.rem(z + d, NZ)
        return copy(bchip.at[rows_of(to)], bbuf.at[z], b_s.at[d], b_r.at[d], zpeer(d))

    for d in order:
        b_copy(d).start()
    bbuf[z] = bchip[rows_of(z)]

    for d in range(1, NX):
        ar_copy(ar_c, yfrom(d), 8 + d, ypeer(d)).wait_recv()
        ar_copy(ar_d, xfrom(d), 12 + d, xpeer(d)).wait_recv()
    low = (ar_c[0] + ar_c[1]) + (ar_c[2] + ar_c[3])
    high = (ar_d[0] + ar_d[1]) + (ar_d[2] + ar_d[3])
    mine_rows = pl.ds(pl.multiple_of(q * H + z * Q, Q), Q)

    sums = [low[0], low[1], high[0], high[1]]
    forward = []
    for t in range(TOP):
        value = nt(trt[t, mine_rows] - sums[t], (tih[t], til[t]))
        if t > 0:
            value = value - nt(forward[-1], (kh[t - 1], kl[t - 1]))
        forward.append(value)
    above = None
    found = [None] * TOP
    for t in reversed(range(TOP)):
        value = nn(forward[t], (tih[t], til[t]))
        if t < TOP - 1:
            value = value - nn(above, (lh[t], ll[t]))
        above = value
        found[t] = value
        topx[t] = value

    def tp_copy(d):
        return copy(topx, topt.at[:, mine_rows], tp_s.at[d], tp_r.at[d], zpeer(d))

    for d in order:
        tp_copy(d).start()
    topt[:, mine_rows] = topx[...]

    found_h, found_l = split(jnp.concatenate(found, axis=1))
    picked = once(found_h, pall[...], ((1,), (0,))) + once(found_l, pall[...], ((1,), (0,)))
    for d in order:
        copy(bchip.at[pl.ds(0, Q)], bbuf.at[zfrom(d)], b_s.at[d], b_r.at[d], zpeer(d)).wait_recv()
    for c in range(NZ):
        reach = jnp.concatenate([vbuf[c, 0, pl.ds(0, 64)], vbuf[c, 1, pl.ds(0, 64)]], axis=0)
        z0[c] = bbuf[c] - nn(picked[:, c * H : (c + 1) * H], reach)

    def back(i, carry):
        c = NZ - 1 - i
        z0[c] = z0[c] + nt(z0[c + 1], (ach[c], acl[c]))
        return carry

    lax.fori_loop(1, NZ, back, 0)

    swap_t = copy(topt.at[:, half], topt.at[:, half], up_s.at[1], up_r.at[1], sibling)
    swap_b = swap(mb_s, mb_r, 4)

    def with_top():
        for d in order:
            place = pl.ds(pl.multiple_of(q * H + zfrom(d) * Q, Q), Q)
            copy(topx, topt.at[:, place], tp_s.at[d], tp_r.at[d], zpeer(d)).wait_recv()
        swap_t.start()
        copy(topt.at[:, other], topt.at[:, other], up_s.at[1], up_r.at[1], sibling).wait_recv()
        pick, pick_chain = 0.0, 0.0
        for t in range(TOP):
            here = pl.ds(t * W, W)
            value = topt[t].T
            top_out[t] = value
            vh, vl = split(value)
            near, far = pt[pl.ds(0, 512), here], pt[pl.ds(512, 64), here]
            pick = pick + (once(near, vh, ((1,), (0,))) + once(near, vl, ((1,), (0,))))
            pick_chain = pick_chain + (once(far, vh, ((1,), (0,))) + once(far, vl, ((1,), (0,))))
        ycat[...] = pick
        bt[...] = bt[...] - tn(pick_chain, side_v[...])
        mb_s[...] = nn(bt[...], a0[...])
        swap_b.start()

        def lower(k):
            hval[k] = hval[k] - tn((n1h[k], n1l[k]), ycat[pl.ds(pl.multiple_of(k * 64, 64), 64)])

        by_four(lower)

    @pl.when(x == 0)
    def _():
        with_top()

    hop_b = copy(xout_b, xin_b, xb_s.at[0], xb_r.at[0], at(lax.rem(x + NX - 1, NX), z, q))

    @pl.when(x == NX - 1)
    def _():
        xin_b[...] = jnp.zeros((Q, W), F32)
        xout_b[...] = z0[0]

    @pl.when(x < NX - 1)
    def _():
        hop_b.wait_recv()
        xout_b[...] = z0[0] + nt(xin_b[...], (fh[NZ - 1], fl[NZ - 1]))

    @pl.when(x > 0)
    def _():
        hop_b.start()

    leaving = split(xin_b[...])
    xsend[NZ - 1] = xin_b[...]

    def unfix(c, carry):
        xsend[c] = z0[c + 1] + nt(leaving, (gh[c + 1], gl[c + 1]))
        return carry

    lax.fori_loop(0, NZ - 1, unfix, 0)

    def xa_copy(d):
        to = lax.rem(z + d, NZ)
        return copy(xsend.at[to], xback.at[rows_of(z)], xa_s.at[d], xa_r.at[d], zpeer(d))

    for d in order:
        xa_copy(d).start()
    xback[rows_of(z)] = xsend[z]

    @pl.when(x > 0)
    def _():
        with_top()

    top_store = pltpu.make_async_copy(top_out, top_to, store.at[LOC + 1])
    top_store.start()
    swap_b.wait_recv()
    base = bt[...] + jnp.where(first, mb_r[...], 0.0)
    for d in order:
        copy(xsend.at[0], xback.at[rows_of(zfrom(d))], xa_s.at[d], xa_r.at[d], zpeer(d)).wait_recv()
    swap_x = swap(xback, zbuf, 5)
    swap_x.start()
    swap_x.wait_recv()
    mine, theirs = xback[...], zbuf[...]
    exits = jnp.concatenate([jnp.where(first, mine, theirs), jnp.where(first, theirs, mine)], axis=0)
    out[LOC] = (base + nn(exits, msel[...])).T

    def keep(k):
        return pltpu.make_async_copy(out.at[k], out_to.at[k], store.at[k])

    keep(LOC).start()
    for k in reversed(range(LOC)):
        out[k] = hval[k] - tn((dh[k], dl[k]), out[links[0, k]])
        keep(k).start()
    for k in range(LOC + 1):
        keep(k).wait()
    top_store.wait()

    for d in order:
        v_copy(d).wait_send()
        v_pass(d).wait_send()
        s_copy(d).wait_send()
        zr_copy(d).wait_send()
        zb_copy(d).wait_send()
        b_copy(d).wait_send()
        tp_copy(d).wait_send()
        xa_copy(d).wait_send()
    v_own.wait_send()
    for step in moves:
        for move in step:
            ring(*move).wait_send()
            ring_pass(*move).wait_send()
    for item in (swap_a, swap_s, swap_u, swap_z, swap_m, swap_t, swap_b, swap_x):
        item.wait_send()
    for d in range(1, NX):
        y_copy(d).wait_send()
        ar_copy(ar_a, x, d, xpeer(d)).wait_send()
        ar_copy(ar_b, leaf, 4 + d, ypeer(d)).wait_send()
        ar_copy(ar_c, leaf, 8 + d, ypeer(d)).wait_send()
        ar_copy(ar_d, x, 12 + d, xpeer(d)).wait_send()

    @pl.when(x < NX - 1)
    def _():
        hop_f.wait_send()

    @pl.when(x > 0)
    def _():
        hop_b.wait_send()


def shards(
    node_rhs, node_inverse, local_blocks, chain_next, chain_top, top_rhs, top_inverse, top_next,
    ancestors, block_rows, chain_target, chain_rows,
):
    vmem = pl.BlockSpec(memory_space=pltpu.VMEM)
    smem = pl.BlockSpec(memory_space=pltpu.SMEM)
    hbm = pl.BlockSpec(memory_space=pl.ANY)

    def f32(*shape):
        return pltpu.VMEM(shape, F32)

    def b16(*shape):
        return pltpu.VMEM(shape, BF16)

    def sem(count):
        return pltpu.SemaphoreType.DMA((count,))

    scratch = [
        f32(LOC + 1, W, W), f32(LOC + 1, W, W), f32(LOC, 128, W), f32(TOP, W, W), f32(TOP, W, W),
        f32(TOP - 1, W, W), f32(LOC + 1, W, W), f32(TOP, W, W),
        b16(LOC, W, W), b16(LOC, W, W), b16(LOC, 64, W), b16(LOC, 64, W), f32(512, W), b16(576, TOP * W),
        f32(LOC, W, W), f32(TOP, W, W), f32(TOP, H, W), f32(TOP, H, W), f32(NY, H, W), f32(H, W), f32(NZ, Q, W),
        f32(W, W), f32(W, W), f32(W, W), f32(W, W), f32(W, W), f32(64, W),
        f32(NZ, W, W), b16(NZ, W, W), b16(NZ, W, W), b16(NZ, W, W), b16(NZ, W, W), b16(NZ, W, W), b16(NZ, W, W),
        f32(NZ, 2, 72, W), b16(TOP * W, NZ * H),
        f32(W, W), f32(W, W), f32(W, W), f32(H, W), f32(NZ, Q, W), f32(NZ, Q, W), f32(NZ, Q, W), f32(H, W),
        f32(H, W), f32(Q, W), f32(Q, W),
        f32(NX, 2, Q, W), f32(NY, 2, Q, W), f32(NY, 2, Q, W), f32(NX, 2, Q, W),
        f32(TOP, Q, W), f32(TOP, W, W), f32(TOP, W, W), b16(TOP, W, W), b16(TOP, W, W),
        b16(TOP - 1, W, W), b16(TOP - 1, W, W), b16(TOP - 1, W, W), b16(TOP - 1, W, W),
        f32(W, W), f32(W, W), f32(W, W), f32(H, W), f32(NZ, Q, W), f32(NZ, Q, W), f32(H, W),
        f32(Q, W), f32(Q, W), f32(W, W), f32(W, W),
        sem(7), sem(LOC + 2), sem(6), sem(6), sem(16), sem(16), sem(16), sem(16), sem(8), sem(8), sem(8), sem(8),
        sem(1), sem(1),
        sem(8), sem(8), sem(2), sem(2), sem(4), sem(4), sem(8), sem(8), sem(1), sem(1), sem(8), sem(8),
        sem(16), sem(16), sem(8), sem(8), sem(1), sem(1), sem(8), sem(8), sem(8), sem(8),
    ]
    solved, top = pl.pallas_call(
        kernel,
        out_shape=(
            jax.ShapeDtypeStruct((LOC + 1, W, W), F32),
            jax.ShapeDtypeStruct((TOP, W, W), F32),
        ),
        in_specs=[smem, smem, hbm, hbm, hbm, vmem, vmem, hbm, hbm, hbm, vmem, vmem],
        out_specs=(hbm, hbm),
        scratch_shapes=scratch,
        compiler_params=pltpu.CompilerParams(
            collective_id=0, has_side_effects=True, vmem_limit_bytes=56 * 1024 * 1024
        ),
    )(
        ancestors[0, 0].T,
        chain_target[0],
        node_rhs[0, 0],
        node_inverse[0, 0],
        local_blocks[0, 0].reshape(LOC, 128, W),
        chain_next[0, 0],
        chain_top[0, 0],
        top_rhs,
        top_inverse,
        top_next,
        block_rows[0, 0].reshape(2 * LOC, 64),
        chain_rows[0],
    )
    return solved[None, None], top


def solution(mesh):
    placed = (
        P("leaf", "col", None, None, None),
        P("leaf", "col", None, None, None),
        P("leaf", "col", None, None, None, None),
        P("leaf", "col", None, None),
        P("leaf", "col", None, None),
        P(),
        P(),
        P(),
        P("leaf", "col", None, None),
        P("leaf", "col", None, None, None),
        P("leaf", "col"),
        P("leaf", "col", None),
    )
    return jax.shard_map(
        shards,
        mesh=mesh,
        in_specs=placed,
        out_specs=(P("leaf", "col", None, None, None), P()),
        check_vma=False,
    )
```

```python
import jax
import jax.numpy as jnp
from jax import lax
from jax.experimental import pallas as pl
from jax.experimental.pallas import tpu as pltpu
from jax.sharding import PartitionSpec as P

F32 = jnp.float32
BF16 = jnp.bfloat16
MESH = pl.DeviceIdType.MESH
NX, NZ, NY, NCOL = 4, 8, 4, 64
W = 256
H = 128
Q = 16
LOC = 8
TOP = 4


def split(value):
    if isinstance(value, tuple):
        return value
    high = value.astype(BF16)
    return high, (value - high.astype(F32)).astype(BF16)


def once(left, right, dims):
    return lax.dot_general(left, right, (dims, ((), ())), preferred_element_type=F32)


def thrice(left, right, dims):
    lh, ll = split(left)
    rh, rl = split(right)
    return once(lh, rh, dims) + (once(lh, rl, dims) + once(ll, rh, dims))


def nn(left, right):
    return thrice(left, right, ((1,), (0,)))


def nt(left, right):
    return thrice(left, right, ((1,), (1,)))


def tn(left, right):
    return thrice(left, right, ((0,), (0,)))


def one_hot(index_row, extent):
    place = lax.broadcasted_iota(jnp.int32, (extent, index_row.shape[1]), 0)
    return jnp.where(place == index_row, 1.0, 0.0).astype(BF16)


def kernel(
    links, target, rhs_in, inverse_in, blocks_in, onward, sideways, top_rhs_in, top_inverse_in, top_next_in, rows, chain_rows,
    out_to, top_to,
    src, inverse, blocks, top_rhs, top_inverse, top_next, out, top_out,
    dh, dl, n1h, n1l, ycat, pt, hval, upt, uprecv, uph, ybuf, uy, zred,
    a_own, a_sib, a0, a1, msel, side_v, acf, ach, acl, fh, fl, gh, gl, vbuf, pall,
    rt, ex_s, ex_r, schip, sbuf, z0, zsend, zbuf, zback, xin_f, xout_f,
    ar_a, ar_b, ar_c, ar_d, topx, topt, trt, tih, til, kh, kl, lh, ll,
    bt, m_s, m_r, bchip, bbuf, xsend, xback, xin_b, xout_b, mb_s, mb_r,
    load, store, core_s, core_r, ac_s, ac_r, acx_s, acx_r, v_s, v_r, vx_s, vx_r, vo_s, vo_r,
    s_s, s_r, up_s, up_r, y_s, y_r, zr_s, zr_r, xf_s, xf_r, zb_s, zb_r, ar_s, ar_r,
    b_s, b_r, xb_s, xb_r, xa_s, xa_r, tp_s, tp_r,
):
    leaf = lax.axis_index("leaf")
    col = lax.axis_index("col")
    x, z, q = col // 16, (col // 2) % NZ, col % 2

    def at(xx, zz, qq):
        return (leaf, xx * 16 + zz * 2 + qq)

    sibling = at(x, z, 1 - q)

    def zpeer(d):
        return at(x, lax.rem(z + d, NZ), q)

    def xpeer(d):
        return at(lax.rem(x + d, NX), z, q)

    def ypeer(d):
        return (lax.rem(leaf + d, NY), col)

    def zfrom(d):
        return lax.rem(z + NZ - d, NZ)

    def xfrom(d):
        return lax.rem(x + NX - d, NX)

    def yfrom(d):
        return lax.rem(leaf + NY - d, NY)

    def copy(source, goal, ss, rs, device):
        return pltpu.make_async_remote_copy(
            src_ref=source, dst_ref=goal, send_sem=ss, recv_sem=rs, device_id=device, device_id_type=MESH
        )

    def swap(source, goal, number):
        return copy(source, goal, core_s.at[number], core_r.at[number], sibling)

    barrier = pltpu.get_barrier_semaphore()
    peers = [sibling] + [zpeer(d) for d in range(1, NZ)] + [xpeer(d) for d in range(1, NX)]
    peers = peers + [ypeer(d) for d in range(1, NY)]
    for peer in peers:
        pl.semaphore_signal(barrier, inc=1, device_id=peer, device_id_type=MESH)

    loads = [
        pltpu.make_async_copy(inverse_in.at[LOC], inverse.at[LOC], load.at[0]),
        pltpu.make_async_copy(inverse_in.at[pl.ds(0, LOC)], inverse.at[pl.ds(0, LOC)], load.at[1]),
        pltpu.make_async_copy(blocks_in, blocks, load.at[2]),
        pltpu.make_async_copy(rhs_in, src, load.at[3]),
        pltpu.make_async_copy(top_inverse_in, top_inverse, load.at[4]),
        pltpu.make_async_copy(top_next_in, top_next, load.at[5]),
        pltpu.make_async_copy(top_rhs_in, top_rhs, load.at[6]),
    ]
    for item in loads:
        item.start()

    first = q == 0
    half = pl.ds(pl.multiple_of(q * H, H), H)
    other = pl.ds(pl.multiple_of((1 - q) * H, H), H)

    def rows_of(zz):
        return pl.ds(pl.multiple_of(zz * Q, Q), Q)

    def by_four(body):
        def four(i, carry):
            for j in range(4):
                body(4 * i + j)
            return carry

        lax.fori_loop(0, 2, four, 0)

    loads[0].wait()
    chain_inverse = split(inverse[LOC])
    coupling = jnp.where(col == NCOL - 1, jnp.zeros((W, W), F32), onward[...])
    a_own[...] = -nn(coupling, chain_inverse)
    pl.semaphore_wait(barrier, len(peers))
    swap_a = swap(a_own, a_sib, 0)
    swap_a.start()
    side = nn(sideways[...], chain_inverse)
    side_v[...] = side
    loads[1].wait()
    loads[2].wait()

    def local_map(k):
        near = nn(blocks[k], inverse[k])
        near_h, near_l = split(near)
        to_parent = one_hot(rows[pl.ds(2 * k, 1), :], W)
        dh[k] = once(to_parent, near_h[:64], ((1,), (0,))).astype(BF16)
        dl[k] = once(to_parent, near_l[:64], ((1,), (0,))).astype(BF16)
        n1h[k] = near_h[64:]
        n1l[k] = near_l[64:]

    def some_maps(start):
        def two(i, carry):
            local_map(start + 2 * i)
            local_map(start + 2 * i + 1)
            return carry

        lax.fori_loop(0, 2, two, 0)

    swap_a.wait_recv()
    a0[...] = jnp.where(first, a_own[...], a_sib[...])
    a1[...] = jnp.where(first, a_sib[...], a_own[...])
    pair = nn(a1[...], a0[...])
    acf[z] = pair.T

    def ring_part(core, way, s, h):
        slot = lax.rem(z + NZ - s * way, NZ)
        return acf.at[slot, pl.ds(pl.multiple_of(core * H + h * 64, 64), 64)]

    def ring_number(way, s, h):
        return ((way + 1) // 2 * 4 + s) * 2 + h

    def ring(way, s, h):
        part, i = ring_part(q, way, s, h), ring_number(way, s, h)
        return copy(part, part, ac_s.at[i], ac_r.at[i], zpeer(way % NZ))

    def ring_in(way, s, h):
        part, i = ring_part(q, way, s + 1, h), ring_number(way, s, h)
        return copy(part, part, ac_s.at[i], ac_r.at[i], zpeer(way % NZ))

    def ring_pass(way, s, h):
        part, i = ring_part(q, way, s + 1, h), ring_number(way, s, h)
        return copy(part, part, acx_s.at[i], acx_r.at[i], sibling)

    def ring_passed(way, s, h):
        part, i = ring_part(1 - q, way, s + 1, h), ring_number(way, s, h)
        return copy(part, part, acx_s.at[i], acx_r.at[i], sibling)

    moves = [[(way, s, h) for h in range(2) for way in (1, -1)] for s in range(3)]
    moves.append([(1, 3, 0), (-1, 3, 1)])

    def ring_step(s):
        if s > 0:
            for way, _, h in moves[s - 1]:
                ring_in(way, s - 1, h).wait_recv()
                if s < 4 and (way, s, h) in moves[s]:
                    ring(way, s, h).start()
                ring_pass(way, s - 1, h).start()
        else:
            for way, _, h in moves[0]:
                ring(way, 0, h).start()

    ring_step(0)
    msel[...] = jnp.where(first, pair, a_own[...])
    vbuf[z, q, pl.ds(0, 64)] = jnp.where(first, side, nn(side, a0[...]))
    index = (chain_rows[...] + target[0] * W).astype(F32)
    empty = jnp.zeros((1, 64), F32)
    index = jnp.concatenate(
        [jnp.where(first, index, empty), jnp.where(first, empty, index), jnp.zeros((1, 128), F32)], axis=1
    )
    vbuf[z, q, pl.ds(64, 8)] = jnp.broadcast_to(index, (8, W))

    def v_copy(d):
        return copy(vbuf.at[z, q], vbuf.at[z, q], v_s.at[d], v_r.at[d], zpeer(d))

    order = (1, 7, 2, 6, 3, 5, 4)
    v_own = copy(vbuf.at[z, q], vbuf.at[z, q], vo_s.at[0], vo_r.at[0], sibling)
    v_own.start()
    some_maps(0)
    ring_step(1)
    some_maps(4)
    ring_step(2)
    loads[3].wait()

    for k in range(LOC):
        update = nn((dh[k], dl[k]), src[k])
        for j in range(k + 1, LOC + 1):
            src[j] = src[j] - jnp.where(links[0, k] == j, update, 0.0)

    ring_step(3)
    rt[...] = src[LOC].T
    ex_s[...] = jnp.where(first, -nt(rt[...], a_own[...]), rt[...])
    swap_s = swap(ex_s, ex_r, 1)
    swap_s.start()
    swap_s.wait_recv()
    shift_half = jnp.where(first, ex_s[half], ex_r[half])
    rest_half = jnp.where(first, ex_r[half], ex_s[half])
    schip[...] = -nt(rest_half - shift_half, a1[...])

    def s_copy(d):
        to = lax.rem(z + d, NZ)
        return copy(schip.at[rows_of(to)], sbuf.at[z], s_s.at[d], s_r.at[d], zpeer(d))

    for d in order:
        s_copy(d).start()
    sbuf[z] = schip[rows_of(z)]

    for d in order:
        v_copy(d).start()

    ring_step(4)

    def up_part(k):
        ycat[pl.ds(pl.multiple_of(k * 64, 64), 64)] = nn((n1h[k], n1l[k]), src[k])

    by_four(up_part)
    diagonal = lax.broadcasted_iota(jnp.int32, (64, 64), 0) == lax.broadcasted_iota(jnp.int32, (64, 64), 1)

    def places_of(index_row):
        column = jnp.sum(jnp.where(diagonal, index_row, 0.0), axis=1, keepdims=True).astype(jnp.int32)
        place = lax.broadcasted_iota(jnp.int32, (64, TOP * W), 1)
        return jnp.where(place == column, 1.0, 0.0).astype(BF16)

    def places_body(k):
        index_row = (rows[pl.ds(2 * k + 1, 1), :] + links[1, k] * W).astype(F32)
        pt[pl.ds(pl.multiple_of(k * 64, 64), 64)] = places_of(index_row)

    by_four(places_body)
    pt[pl.ds(512, 64)] = places_of((chain_rows[...] + target[0] * W).astype(F32))
    up_h, up_l = split(ycat[...].T)
    chain_h, chain_l = split(nt(jnp.where(first, rt[...], rt[...] - ex_r[...]), side_v[...]))
    for t in range(TOP):
        here = pl.ds(t * W, W)
        near, far = pt[pl.ds(0, 512), here], pt[pl.ds(512, 64), here]
        near = once(up_h, near, ((1,), (0,))) + once(up_l, near, ((1,), (0,)))
        far = once(chain_h, far, ((1,), (0,))) + once(chain_l, far, ((1,), (0,)))
        upt[t] = near + far
    swap_u = copy(upt.at[:, other], uprecv, up_s.at[0], up_r.at[0], sibling)
    swap_u.start()

    for item in loads[4:]:
        item.wait()
    for t in range(TOP):
        th, tl = split(top_inverse[t])
        tih[t] = th
        til[t] = tl
        trt[t] = top_rhs[t].T
    for t in range(TOP - 1):
        kh[t], kl[t] = split(nn((tih[t + 1], til[t + 1]), top_next[t]))
        lh[t], ll[t] = split(nn(top_next[t], (tih[t], til[t])))
    swap_u.wait_recv()
    for t in range(TOP):
        uph[t] = upt[t, half] + uprecv[t]

    def y_copy(d):
        return copy(uph.at[lax.rem(leaf + d, NY)], ybuf.at[leaf], y_s.at[d], y_r.at[d], ypeer(d))

    for d in range(1, NY):
        y_copy(d).start()
    ybuf[leaf] = uph[leaf]

    def square(k):
        here = split(inverse[k])
        hval[k] = tn(here, nn(here, src[k]))

    def v_come(d):
        part = vbuf.at[zfrom(d), q]
        return copy(part, part, v_s.at[d], v_r.at[d], zpeer(d))

    def v_pass(d):
        part = vbuf.at[zfrom(d), q]
        return copy(part, part, vx_s.at[d], vx_r.at[d], sibling)

    def v_passed(d):
        part = vbuf.at[zfrom(d), 1 - q]
        return copy(part, part, vx_s.at[d], vx_r.at[d], sibling)

    for step in moves:
        for move in step:
            ring_passed(*move).wait_recv()

    def halves(c, carry):
        ach[c], acl[c] = split(acf[c])
        return carry

    lax.fori_loop(0, NZ, halves, 0)
    for d in order:
        copy(schip.at[pl.ds(0, Q)], sbuf.at[zfrom(d)], s_s.at[d], s_r.at[d], zpeer(d)).wait_recv()

    z0[0] = sbuf[0]
    fh[0] = ach[0]
    fl[0] = acl[0]

    def prefix(c, carry):
        here = (ach[c], acl[c])
        z0[c] = sbuf[c] + nn(z0[c - 1], here)
        fh[c], fl[c] = split(nn((fh[c - 1], fl[c - 1]), here))
        return carry

    lax.fori_loop(1, NZ, prefix, 0)

    def zr_copy(d):
        to = lax.rem(z + d, NZ)
        return copy(uy.at[rows_of(to)], zred.at[z], zr_s.at[d], zr_r.at[d], zpeer(d))

    def aside():
        for d in range(1, NY):
            copy(uph.at[0], ybuf.at[yfrom(d)], y_s.at[d], y_r.at[d], ypeer(d)).wait_recv()
        uy[...] = (ybuf[0] + ybuf[1]) + (ybuf[2] + ybuf[3])
        for d in order:
            zr_copy(d).start()
        zred[z] = uy[rows_of(z)]
        by_four(square)

    @pl.when(x >= 2)
    def _():
        aside()

    whole = (fh[NZ - 1], fl[NZ - 1])
    hop_f = copy(xout_f, xin_f, xf_s.at[0], xf_r.at[0], at(lax.rem(x + 1, NX), z, q))

    @pl.when(x == 0)
    def _():
        xin_f[...] = jnp.zeros((Q, W), F32)
        xout_f[...] = z0[NZ - 1]

    @pl.when(x > 0)
    def _():
        hop_f.wait_recv()
        xout_f[...] = z0[NZ - 1] + nn(xin_f[...], whole)

    @pl.when(x < NX - 1)
    def _():
        hop_f.start()

    @pl.when(x < 2)
    def _():
        aside()

    entering = split(xin_f[...])
    zsend[0] = xin_f[...]

    def fix(c, carry):
        zsend[c] = z0[c - 1] + nn(entering, (fh[c - 1], fl[c - 1]))
        return carry

    lax.fori_loop(1, NZ, fix, 0)

    def zb_copy(d):
        to = lax.rem(z + d, NZ)
        return copy(zsend.at[to], zback.at[rows_of(z)], zb_s.at[d], zb_r.at[d], zpeer(d))

    for d in order:
        zb_copy(d).start()
    zback[rows_of(z)] = zsend[z]

    for d in order:
        v_come(d).wait_recv()
        v_pass(d).start()
    v_own_come = copy(vbuf.at[z, 1 - q], vbuf.at[z, 1 - q], vo_s.at[0], vo_r.at[0], sibling)
    v_own_come.wait_recv()
    for d in order:
        v_passed(d).wait_recv()

    flows = []
    for c in range(NZ):
        found = (vbuf[c, 0, pl.ds(64, 1), pl.ds(0, H)] + vbuf[c, 1, pl.ds(64, 1), pl.ds(0, H)]).astype(jnp.int32)
        pall[:, c * H : (c + 1) * H] = one_hot(found, TOP * W)
        reach = jnp.concatenate([vbuf[c, 0, pl.ds(0, 64)], vbuf[c, 1, pl.ds(0, 64)]], axis=0)
        flows.append(nt(zsend[c], reach))
    flow_h, flow_l = split(jnp.concatenate(flows, axis=1))
    for d in order:
        copy(uy.at[pl.ds(0, Q)], zred.at[zfrom(d)], zr_s.at[d], zr_r.at[d], zpeer(d)).wait_recv()
    reduced = zred[0]
    for c in range(1, NZ):
        reduced = reduced + zred[c]
    for t in range(TOP):
        places = pall[t * W : (t + 1) * W, :]
        down = once(flow_h, places, ((1,), (1,))) + once(flow_l, places, ((1,), (1,)))
        part = jnp.where(leaf == t, reduced, 0.0) - down
        if t < 2:
            ar_a[x, t] = part
        else:
            ar_b[leaf, t - 2] = part

    def ar_copy(buf, mine, number, device):
        return copy(buf.at[mine], buf.at[mine], ar_s.at[number], ar_r.at[number], device)

    for d in range(1, NX):
        ar_copy(ar_a, x, d, xpeer(d)).start()
        ar_copy(ar_b, leaf, 4 + d, ypeer(d)).start()

    gh[NZ - 1] = ach[NZ - 1]
    gl[NZ - 1] = acl[NZ - 1]

    def suffix(i, carry):
        c = NZ - 1 - i
        gh[c], gl[c] = split(nn((ach[c], acl[c]), (gh[c + 1], gl[c + 1])))
        return carry

    lax.fori_loop(1, NZ, suffix, 0)

    for d in order:
        copy(zsend.at[0], zback.at[rows_of(zfrom(d))], zb_s.at[d], zb_r.at[d], zpeer(d)).wait_recv()
    swap_z = swap(zback, zbuf, 2)
    swap_z.start()

    for d in range(1, NX):
        ar_copy(ar_a, xfrom(d), d, xpeer(d)).wait_recv()
        ar_copy(ar_b, yfrom(d), 4 + d, ypeer(d)).wait_recv()
    ar_c[leaf] = (ar_a[0] + ar_a[1]) + (ar_a[2] + ar_a[3])
    ar_d[x] = (ar_b[0] + ar_b[1]) + (ar_b[2] + ar_b[3])
    for d in range(1, NX):
        ar_copy(ar_c, leaf, 8 + d, ypeer(d)).start()
        ar_copy(ar_d, x, 12 + d, xpeer(d)).start()

    swap_z.wait_recv()
    mine, theirs = zback[...], zbuf[...]
    entry = jnp.concatenate([jnp.where(first, mine, theirs), jnp.where(first, theirs, mine)], axis=0)
    inner = ex_r[...] + nt(entry, a0[...])
    entry = jnp.where(first, entry, inner)
    chain_inverse = split(inverse[LOC])
    bt[...] = nn(nt(rt[...] - entry, chain_inverse), chain_inverse)
    m_s[...] = jnp.where(first, bt[...], nn(bt[...], a0[...]))
    swap_m = swap(m_s, m_r, 3)
    swap_m.start()
    swap_m.wait_recv()
    bchip[...] = m_s[half] + m_r[half]

    def b_copy(d):
        to = lax.rem(z + d, NZ)
        return copy(bchip.at[rows_of(to)], bbuf.at[z], b_s.at[d], b_r.at[d], zpeer(d))

    for d in order:
        b_copy(d).start()
    bbuf[z] = bchip[rows_of(z)]

    for d in range(1, NX):
        ar_copy(ar_c, yfrom(d), 8 + d, ypeer(d)).wait_recv()
        ar_copy(ar_d, xfrom(d), 12 + d, xpeer(d)).wait_recv()
    low = (ar_c[0] + ar_c[1]) + (ar_c[2] + ar_c[3])
    high = (ar_d[0] + ar_d[1]) + (ar_d[2] + ar_d[3])
    mine_rows = pl.ds(pl.multiple_of(q * H + z * Q, Q), Q)

    sums = [low[0], low[1], high[0], high[1]]
    forward = []
    for t in range(TOP):
        value = nt(trt[t, mine_rows] - sums[t], (tih[t], til[t]))
        if t > 0:
            value = value - nt(forward[-1], (kh[t - 1], kl[t - 1]))
        forward.append(value)
    above = None
    found = [None] * TOP
    for t in reversed(range(TOP)):
        value = nn(forward[t], (tih[t], til[t]))
        if t < TOP - 1:
            value = value - nn(above, (lh[t], ll[t]))
        above = value
        found[t] = value
        topx[t] = value

    def tp_copy(d):
        return copy(topx, topt.at[:, mine_rows], tp_s.at[d], tp_r.at[d], zpeer(d))

    for d in order:
        tp_copy(d).start()
    topt[:, mine_rows] = topx[...]

    found_h, found_l = split(jnp.concatenate(found, axis=1))
    picked = once(found_h, pall[...], ((1,), (0,))) + once(found_l, pall[...], ((1,), (0,)))
    for d in order:
        copy(bchip.at[pl.ds(0, Q)], bbuf.at[zfrom(d)], b_s.at[d], b_r.at[d], zpeer(d)).wait_recv()
    for c in range(NZ):
        reach = jnp.concatenate([vbuf[c, 0, pl.ds(0, 64)], vbuf[c, 1, pl.ds(0, 64)]], axis=0)
        z0[c] = bbuf[c] - nn(picked[:, c * H : (c + 1) * H], reach)

    def back(i, carry):
        c = NZ - 1 - i
        z0[c] = z0[c] + nt(z0[c + 1], (ach[c], acl[c]))
        return carry

    lax.fori_loop(1, NZ, back, 0)

    swap_t = copy(topt.at[:, half], topt.at[:, half], up_s.at[1], up_r.at[1], sibling)
    swap_b = swap(mb_s, mb_r, 4)

    def with_top():
        for d in order:
            v_copy(d).wait_send()
            v_pass(d).wait_send()
            s_copy(d).wait_send()
            zr_copy(d).wait_send()
            zb_copy(d).wait_send()
            b_copy(d).wait_send()
        v_own.wait_send()
        for step in moves:
            for move in step:
                ring(*move).wait_send()
                ring_pass(*move).wait_send()
        for item in (swap_a, swap_s, swap_u, swap_z, swap_m):
            item.wait_send()
        for d in range(1, NX):
            y_copy(d).wait_send()
            ar_copy(ar_a, x, d, xpeer(d)).wait_send()
            ar_copy(ar_b, leaf, 4 + d, ypeer(d)).wait_send()
            ar_copy(ar_c, leaf, 8 + d, ypeer(d)).wait_send()
            ar_copy(ar_d, x, 12 + d, xpeer(d)).wait_send()

        @pl.when(x < NX - 1)
        def _():
            hop_f.wait_send()

        for d in order:
            place = pl.ds(pl.multiple_of(q * H + zfrom(d) * Q, Q), Q)
            copy(topx, topt.at[:, place], tp_s.at[d], tp_r.at[d], zpeer(d)).wait_recv()
        swap_t.start()
        copy(topt.at[:, other], topt.at[:, other], up_s.at[1], up_r.at[1], sibling).wait_recv()
        pick, pick_chain = 0.0, 0.0
        for t in range(TOP):
            here = pl.ds(t * W, W)
            value = topt[t].T
            top_out[t] = value
            vh, vl = split(value)
            near, far = pt[pl.ds(0, 512), here], pt[pl.ds(512, 64), here]
            pick = pick + (once(near, vh, ((1,), (0,))) + once(near, vl, ((1,), (0,))))
            pick_chain = pick_chain + (once(far, vh, ((1,), (0,))) + once(far, vl, ((1,), (0,))))
        ycat[...] = pick
        bt[...] = bt[...] - tn(pick_chain, side_v[...])
        mb_s[...] = nn(bt[...], a0[...])
        swap_b.start()

        def lower(k):
            hval[k] = hval[k] - tn((n1h[k], n1l[k]), ycat[pl.ds(pl.multiple_of(k * 64, 64), 64)])

        by_four(lower)

    @pl.when(x == 0)
    def _():
        with_top()

    hop_b = copy(xout_b, xin_b, xb_s.at[0], xb_r.at[0], at(lax.rem(x + NX - 1, NX), z, q))

    @pl.when(x == NX - 1)
    def _():
        xin_b[...] = jnp.zeros((Q, W), F32)
        xout_b[...] = z0[0]

    @pl.when(x < NX - 1)
    def _():
        hop_b.wait_recv()
        xout_b[...] = z0[0] + nt(xin_b[...], (fh[NZ - 1], fl[NZ - 1]))

    @pl.when(x > 0)
    def _():
        hop_b.start()

    leaving = split(xin_b[...])
    xsend[NZ - 1] = xin_b[...]

    def unfix(c, carry):
        xsend[c] = z0[c + 1] + nt(leaving, (gh[c + 1], gl[c + 1]))
        return carry

    lax.fori_loop(0, NZ - 1, unfix, 0)

    def xa_copy(d):
        to = lax.rem(z + d, NZ)
        return copy(xsend.at[to], xback.at[rows_of(z)], xa_s.at[d], xa_r.at[d], zpeer(d))

    for d in order:
        xa_copy(d).start()
    xback[rows_of(z)] = xsend[z]

    @pl.when(x > 0)
    def _():
        with_top()

    top_store = pltpu.make_async_copy(top_out, top_to, store.at[LOC + 1])
    top_store.start()
    swap_b.wait_recv()
    base = bt[...] + jnp.where(first, mb_r[...], 0.0)
    for d in order:
        copy(xsend.at[0], xback.at[rows_of(zfrom(d))], xa_s.at[d], xa_r.at[d], zpeer(d)).wait_recv()
    swap_x = swap(xback, zbuf, 5)
    swap_x.start()
    swap_x.wait_recv()
    mine, theirs = xback[...], zbuf[...]
    exits = jnp.concatenate([jnp.where(first, mine, theirs), jnp.where(first, theirs, mine)], axis=0)
    out[LOC] = (base + nn(exits, msel[...])).T

    def keep(k):
        return pltpu.make_async_copy(out.at[k], out_to.at[k], store.at[k])

    keep(LOC).start()
    for k in reversed(range(LOC)):
        out[k] = hval[k] - tn((dh[k], dl[k]), out[links[0, k]])
        keep(k).start()
    for k in range(LOC + 1):
        keep(k).wait()
    top_store.wait()

    for d in order:
        tp_copy(d).wait_send()
        xa_copy(d).wait_send()
    for item in (swap_t, swap_b, swap_x):
        item.wait_send()

    @pl.when(x > 0)
    def _():
        hop_b.wait_send()


def shards(
    node_rhs, node_inverse, local_blocks, chain_next, chain_top, top_rhs, top_inverse, top_next,
    ancestors, block_rows, chain_target, chain_rows,
):
    vmem = pl.BlockSpec(memory_space=pltpu.VMEM)
    smem = pl.BlockSpec(memory_space=pltpu.SMEM)
    hbm = pl.BlockSpec(memory_space=pl.ANY)

    def f32(*shape):
        return pltpu.VMEM(shape, F32)

    def b16(*shape):
        return pltpu.VMEM(shape, BF16)

    def sem(count):
        return pltpu.SemaphoreType.DMA((count,))

    scratch = [
        f32(LOC + 1, W, W), f32(LOC + 1, W, W), f32(LOC, 128, W), f32(TOP, W, W), f32(TOP, W, W),
        f32(TOP - 1, W, W), f32(LOC + 1, W, W), f32(TOP, W, W),
        b16(LOC, W, W), b16(LOC, W, W), b16(LOC, 64, W), b16(LOC, 64, W), f32(512, W), b16(576, TOP * W),
        f32(LOC, W, W), f32(TOP, W, W), f32(TOP, H, W), f32(TOP, H, W), f32(NY, H, W), f32(H, W), f32(NZ, Q, W),
        f32(W, W), f32(W, W), f32(W, W), f32(W, W), f32(W, W), f32(64, W),
        f32(NZ, W, W), b16(NZ, W, W), b16(NZ, W, W), b16(NZ, W, W), b16(NZ, W, W), b16(NZ, W, W), b16(NZ, W, W),
        f32(NZ, 2, 72, W), b16(TOP * W, NZ * H),
        f32(W, W), f32(W, W), f32(W, W), f32(H, W), f32(NZ, Q, W), f32(NZ, Q, W), f32(NZ, Q, W), f32(H, W),
        f32(H, W), f32(Q, W), f32(Q, W),
        f32(NX, 2, Q, W), f32(NY, 2, Q, W), f32(NY, 2, Q, W), f32(NX, 2, Q, W),
        f32(TOP, Q, W), f32(TOP, W, W), f32(TOP, W, W), b16(TOP, W, W), b16(TOP, W, W),
        b16(TOP - 1, W, W), b16(TOP - 1, W, W), b16(TOP - 1, W, W), b16(TOP - 1, W, W),
        f32(W, W), f32(W, W), f32(W, W), f32(H, W), f32(NZ, Q, W), f32(NZ, Q, W), f32(H, W),
        f32(Q, W), f32(Q, W), f32(W, W), f32(W, W),
        sem(7), sem(LOC + 2), sem(6), sem(6), sem(16), sem(16), sem(16), sem(16), sem(8), sem(8), sem(8), sem(8),
        sem(1), sem(1),
        sem(8), sem(8), sem(2), sem(2), sem(4), sem(4), sem(8), sem(8), sem(1), sem(1), sem(8), sem(8),
        sem(16), sem(16), sem(8), sem(8), sem(1), sem(1), sem(8), sem(8), sem(8), sem(8),
    ]
    solved, top = pl.pallas_call(
        kernel,
        out_shape=(
            jax.ShapeDtypeStruct((LOC + 1, W, W), F32),
            jax.ShapeDtypeStruct((TOP, W, W), F32),
        ),
        in_specs=[smem, smem, hbm, hbm, hbm, vmem, vmem, hbm, hbm, hbm, vmem, vmem],
        out_specs=(hbm, hbm),
        scratch_shapes=scratch,
        compiler_params=pltpu.CompilerParams(
            collective_id=0, has_side_effects=True, vmem_limit_bytes=56 * 1024 * 1024
        ),
    )(
        ancestors[0, 0].T,
        chain_target[0],
        node_rhs[0, 0],
        node_inverse[0, 0],
        local_blocks[0, 0].reshape(LOC, 128, W),
        chain_next[0, 0],
        chain_top[0, 0],
        top_rhs,
        top_inverse,
        top_next,
        block_rows[0, 0].reshape(2 * LOC, 64),
        chain_rows[0],
    )
    return solved[None, None], top


def solution(mesh):
    placed = (
        P("leaf", "col", None, None, None),
        P("leaf", "col", None, None, None),
        P("leaf", "col", None, None, None, None),
        P("leaf", "col", None, None),
        P("leaf", "col", None, None),
        P(),
        P(),
        P(),
        P("leaf", "col", None, None),
        P("leaf", "col", None, None, None),
        P("leaf", "col"),
        P("leaf", "col", None),
    )
    return jax.shard_map(
        shards,
        mesh=mesh,
        in_specs=placed,
        out_specs=(P("leaf", "col", None, None, None), P()),
        check_vma=False,
    )
```

```python
import jax
import jax.numpy as jnp
from jax import lax
from jax.experimental import pallas as pl
from jax.experimental.pallas import tpu as pltpu
from jax.sharding import PartitionSpec as P

F32 = jnp.float32
BF16 = jnp.bfloat16
MESH = pl.DeviceIdType.MESH
NX, NZ, NY, NCOL = 4, 8, 4, 64
W = 256
H = 128
Q = 16
LOC = 8
TOP = 4


def split(value):
    if isinstance(value, tuple):
        return value
    high = value.astype(BF16)
    return high, (value - high.astype(F32)).astype(BF16)


def once(left, right, dims):
    return lax.dot_general(left, right, (dims, ((), ())), preferred_element_type=F32)


def thrice(left, right, dims):
    lh, ll = split(left)
    rh, rl = split(right)
    return once(lh, rh, dims) + (once(lh, rl, dims) + once(ll, rh, dims))


def nn(left, right):
    return thrice(left, right, ((1,), (0,)))


def nt(left, right):
    return thrice(left, right, ((1,), (1,)))


def tn(left, right):
    return thrice(left, right, ((0,), (0,)))


def one_hot(index_row, extent):
    place = lax.broadcasted_iota(jnp.int32, (extent, index_row.shape[1]), 0)
    return jnp.where(place == index_row, 1.0, 0.0).astype(BF16)


def kernel(
    links, target, rhs_in, inverse_in, blocks_in, onward, sideways, top_rhs_in, top_inverse_in, top_next_in, rows, chain_rows,
    out_to, top_to,
    src, inverse, blocks, top_rhs, top_inverse, top_next, out, top_out,
    dh, dl, n1h, n1l, ycat, pt, hval, upt, uprecv, uph, ybuf, uy, zred,
    a_own, a_sib, a0, a1, msel, side_v, acf, ach, acl, fh, fl, gh, gl, vbuf, pall,
    rt, ex_s, ex_r, schip, sbuf, z0, zsend, zbuf, zback, xin_f, xout_f,
    ar_a, ar_b, ar_c, ar_d, topx, topt, trt, tih, til, kh, kl, lh, ll,
    bt, m_s, m_r, bchip, bbuf, xsend, xback, xin_b, xout_b, mb_s, mb_r,
    load, store, core_s, core_r, ac_s, ac_r, acx_s, acx_r, v_s, v_r, vx_s, vx_r, vo_s, vo_r,
    s_s, s_r, up_s, up_r, y_s, y_r, zr_s, zr_r, xf_s, xf_r, zb_s, zb_r, ar_s, ar_r,
    b_s, b_r, xb_s, xb_r, xa_s, xa_r, tp_s, tp_r,
):
    leaf = lax.axis_index("leaf")
    col = lax.axis_index("col")
    x, z, q = col // 16, (col // 2) % NZ, col % 2

    def at(xx, zz, qq):
        return (leaf, xx * 16 + zz * 2 + qq)

    sibling = at(x, z, 1 - q)

    def zpeer(d):
        return at(x, lax.rem(z + d, NZ), q)

    def xpeer(d):
        return at(lax.rem(x + d, NX), z, q)

    def ypeer(d):
        return (lax.rem(leaf + d, NY), col)

    def zfrom(d):
        return lax.rem(z + NZ - d, NZ)

    def xfrom(d):
        return lax.rem(x + NX - d, NX)

    def yfrom(d):
        return lax.rem(leaf + NY - d, NY)

    def copy(source, goal, ss, rs, device):
        return pltpu.make_async_remote_copy(
            src_ref=source, dst_ref=goal, send_sem=ss, recv_sem=rs, device_id=device, device_id_type=MESH
        )

    def swap(source, goal, number):
        return copy(source, goal, core_s.at[number], core_r.at[number], sibling)

    barrier = pltpu.get_barrier_semaphore()
    peers = [sibling] + [zpeer(d) for d in range(1, NZ)] + [xpeer(d) for d in range(1, NX)]
    peers = peers + [ypeer(d) for d in range(1, NY)]
    for peer in peers:
        pl.semaphore_signal(barrier, inc=1, device_id=peer, device_id_type=MESH)

    loads = [
        pltpu.make_async_copy(inverse_in.at[LOC], inverse.at[LOC], load.at[0]),
        pltpu.make_async_copy(inverse_in.at[pl.ds(0, LOC)], inverse.at[pl.ds(0, LOC)], load.at[1]),
        pltpu.make_async_copy(blocks_in, blocks, load.at[2]),
        pltpu.make_async_copy(rhs_in, src, load.at[3]),
        pltpu.make_async_copy(top_inverse_in, top_inverse, load.at[4]),
        pltpu.make_async_copy(top_next_in, top_next, load.at[5]),
        pltpu.make_async_copy(top_rhs_in, top_rhs, load.at[6]),
    ]
    for item in loads:
        item.start()

    first = q == 0
    half = pl.ds(pl.multiple_of(q * H, H), H)
    other = pl.ds(pl.multiple_of((1 - q) * H, H), H)

    def rows_of(zz):
        return pl.ds(pl.multiple_of(zz * Q, Q), Q)

    def by_four(body):
        def four(i, carry):
            for j in range(4):
                body(4 * i + j)
            return carry

        lax.fori_loop(0, 2, four, 0)

    loads[0].wait()
    chain_inverse = split(inverse[LOC])
    coupling = jnp.where(col == NCOL - 1, jnp.zeros((W, W), F32), onward[...])
    a_own[...] = -nn(coupling, chain_inverse)
    pl.semaphore_wait(barrier, len(peers))
    swap_a = swap(a_own, a_sib, 0)
    swap_a.start()
    side = nn(sideways[...], chain_inverse)
    side_v[...] = side
    loads[1].wait()
    loads[2].wait()

    def local_map(k):
        near = nn(blocks[k], inverse[k])
        near_h, near_l = split(near)
        to_parent = one_hot(rows[pl.ds(2 * k, 1), :], W)
        dh[k] = once(to_parent, near_h[:64], ((1,), (0,))).astype(BF16)
        dl[k] = once(to_parent, near_l[:64], ((1,), (0,))).astype(BF16)
        n1h[k] = near_h[64:]
        n1l[k] = near_l[64:]

    def some_maps(start):
        def two(i, carry):
            local_map(start + 2 * i)
            local_map(start + 2 * i + 1)
            return carry

        lax.fori_loop(0, 2, two, 0)

    swap_a.wait_recv()
    a0[...] = jnp.where(first, a_own[...], a_sib[...])
    a1[...] = jnp.where(first, a_sib[...], a_own[...])
    pair = nn(a1[...], a0[...])
    acf[z] = pair.T

    def ring_part(core, way, s, h):
        slot = lax.rem(z + NZ - s * way, NZ)
        return acf.at[slot, pl.ds(pl.multiple_of(core * H + h * 64, 64), 64)]

    def ring_number(way, s, h):
        return ((way + 1) // 2 * 4 + s) * 2 + h

    def ring(way, s, h):
        part, i = ring_part(q, way, s, h), ring_number(way, s, h)
        return copy(part, part, ac_s.at[i], ac_r.at[i], zpeer(way % NZ))

    def ring_in(way, s, h):
        part, i = ring_part(q, way, s + 1, h), ring_number(way, s, h)
        return copy(part, part, ac_s.at[i], ac_r.at[i], zpeer(way % NZ))

    def ring_pass(way, s, h):
        part, i = ring_part(q, way, s + 1, h), ring_number(way, s, h)
        return copy(part, part, acx_s.at[i], acx_r.at[i], sibling)

    def ring_passed(way, s, h):
        part, i = ring_part(1 - q, way, s + 1, h), ring_number(way, s, h)
        return copy(part, part, acx_s.at[i], acx_r.at[i], sibling)

    moves = [[(way, s, h) for h in range(2) for way in (1, -1)] for s in range(3)]
    moves.append([(1, 3, 0), (-1, 3, 1)])

    def ring_step(s):
        if s > 0:
            for way, _, h in moves[s - 1]:
                ring_in(way, s - 1, h).wait_recv()
                if s < 4 and (way, s, h) in moves[s]:
                    ring(way, s, h).start()
                ring_pass(way, s - 1, h).start()
        else:
            for way, _, h in moves[0]:
                ring(way, 0, h).start()

    ring_step(0)
    msel[...] = jnp.where(first, pair, a_own[...])
    vbuf[z, q, pl.ds(0, 64)] = jnp.where(first, side, nn(side, a0[...]))
    index = (chain_rows[...] + target[0] * W).astype(F32)
    empty = jnp.zeros((1, 64), F32)
    index = jnp.concatenate(
        [jnp.where(first, index, empty), jnp.where(first, empty, index), jnp.zeros((1, 128), F32)], axis=1
    )
    vbuf[z, q, pl.ds(64, 8)] = jnp.broadcast_to(index, (8, W))

    def v_copy(d):
        return copy(vbuf.at[z, q], vbuf.at[z, q], v_s.at[d], v_r.at[d], zpeer(d))

    order = (1, 7, 2, 6, 3, 5, 4)
    v_own = copy(vbuf.at[z, q], vbuf.at[z, q], vo_s.at[0], vo_r.at[0], sibling)
    v_own.start()
    some_maps(0)
    ring_step(1)
    some_maps(4)
    ring_step(2)
    loads[3].wait()

    for k in range(LOC):
        update = nn((dh[k], dl[k]), src[k])
        for j in range(k + 1, LOC + 1):
            src[j] = src[j] - jnp.where(links[0, k] == j, update, 0.0)

    ring_step(3)
    rt[...] = src[LOC].T
    ex_s[...] = jnp.where(first, -nt(rt[...], a_own[...]), rt[...])
    swap_s = swap(ex_s, ex_r, 1)
    swap_s.start()
    swap_s.wait_recv()
    shift_half = jnp.where(first, ex_s[half], ex_r[half])
    rest_half = jnp.where(first, ex_r[half], ex_s[half])
    schip[...] = -nt(rest_half - shift_half, a1[...])

    def s_copy(d):
        to = lax.rem(z + d, NZ)
        return copy(schip.at[rows_of(to)], sbuf.at[z], s_s.at[d], s_r.at[d], zpeer(d))

    for d in order:
        s_copy(d).start()
    sbuf[z] = schip[rows_of(z)]

    for d in order:
        v_copy(d).start()

    ring_step(4)

    def up_part(k):
        ycat[pl.ds(pl.multiple_of(k * 64, 64), 64)] = nn((n1h[k], n1l[k]), src[k])

    by_four(up_part)
    diagonal = lax.broadcasted_iota(jnp.int32, (64, 64), 0) == lax.broadcasted_iota(jnp.int32, (64, 64), 1)

    def places_of(index_row):
        column = jnp.sum(jnp.where(diagonal, index_row, 0.0), axis=1, keepdims=True).astype(jnp.int32)
        place = lax.broadcasted_iota(jnp.int32, (64, TOP * W), 1)
        return jnp.where(place == column, 1.0, 0.0).astype(BF16)

    def places_body(k):
        index_row = (rows[pl.ds(2 * k + 1, 1), :] + links[1, k] * W).astype(F32)
        pt[pl.ds(pl.multiple_of(k * 64, 64), 64)] = places_of(index_row)

    by_four(places_body)
    pt[pl.ds(512, 64)] = places_of((chain_rows[...] + target[0] * W).astype(F32))
    up_h, up_l = split(ycat[...].T)
    chain_h, chain_l = split(nt(jnp.where(first, rt[...], rt[...] - ex_r[...]), side_v[...]))
    for t in range(TOP):
        here = pl.ds(t * W, W)
        near, far = pt[pl.ds(0, 512), here], pt[pl.ds(512, 64), here]
        near = once(up_h, near, ((1,), (0,))) + once(up_l, near, ((1,), (0,)))
        far = once(chain_h, far, ((1,), (0,))) + once(chain_l, far, ((1,), (0,)))
        upt[t] = near + far
    swap_u = copy(upt.at[:, other], uprecv, up_s.at[0], up_r.at[0], sibling)
    swap_u.start()

    for item in loads[4:]:
        item.wait()
    for t in range(TOP):
        th, tl = split(top_inverse[t])
        tih[t] = th
        til[t] = tl
        trt[t] = top_rhs[t].T
    for t in range(TOP - 1):
        kh[t], kl[t] = split(nn((tih[t + 1], til[t + 1]), top_next[t]))
        lh[t], ll[t] = split(nn(top_next[t], (tih[t], til[t])))
    swap_u.wait_recv()
    for t in range(TOP):
        uph[t] = upt[t, half] + uprecv[t]

    def y_copy(d):
        return copy(uph.at[lax.rem(leaf + d, NY)], ybuf.at[leaf], y_s.at[d], y_r.at[d], ypeer(d))

    for d in range(1, NY):
        y_copy(d).start()
    ybuf[leaf] = uph[leaf]

    def square(k):
        here = split(inverse[k])
        hval[k] = tn(here, nn(here, src[k]))

    def v_come(d):
        part = vbuf.at[zfrom(d), q]
        return copy(part, part, v_s.at[d], v_r.at[d], zpeer(d))

    def v_pass(d):
        part = vbuf.at[zfrom(d), q]
        return copy(part, part, vx_s.at[d], vx_r.at[d], sibling)

    def v_passed(d):
        part = vbuf.at[zfrom(d), 1 - q]
        return copy(part, part, vx_s.at[d], vx_r.at[d], sibling)

    for step in moves:
        for move in step:
            ring_passed(*move).wait_recv()

    def halves(c, carry):
        ach[c], acl[c] = split(acf[c])
        return carry

    lax.fori_loop(0, NZ, halves, 0)
    for d in order:
        copy(schip.at[pl.ds(0, Q)], sbuf.at[zfrom(d)], s_s.at[d], s_r.at[d], zpeer(d)).wait_recv()

    z0[0] = sbuf[0]
    fh[0] = ach[0]
    fl[0] = acl[0]

    def prefix(c, carry):
        here = (ach[c], acl[c])
        z0[c] = sbuf[c] + nn(z0[c - 1], here)
        fh[c], fl[c] = split(nn((fh[c - 1], fl[c - 1]), here))
        return carry

    lax.fori_loop(1, NZ, prefix, 0)

    @pl.when(x >= 2)
    def _():
        by_four(square)

    whole = (fh[NZ - 1], fl[NZ - 1])
    hop_f = copy(xout_f, xin_f, xf_s.at[0], xf_r.at[0], at(lax.rem(x + 1, NX), z, q))

    @pl.when(x == 0)
    def _():
        xin_f[...] = jnp.zeros((Q, W), F32)
        xout_f[...] = z0[NZ - 1]

    @pl.when(x > 0)
    def _():
        hop_f.wait_recv()
        xout_f[...] = z0[NZ - 1] + nn(xin_f[...], whole)

    @pl.when(x < NX - 1)
    def _():
        hop_f.start()

    for d in range(1, NY):
        copy(uph.at[0], ybuf.at[yfrom(d)], y_s.at[d], y_r.at[d], ypeer(d)).wait_recv()
    uy[...] = (ybuf[0] + ybuf[1]) + (ybuf[2] + ybuf[3])

    def zr_copy(d):
        to = lax.rem(z + d, NZ)
        return copy(uy.at[rows_of(to)], zred.at[z], zr_s.at[d], zr_r.at[d], zpeer(d))

    for d in order:
        zr_copy(d).start()
    zred[z] = uy[rows_of(z)]

    @pl.when(x < 2)
    def _():
        by_four(square)

    entering = split(xin_f[...])
    zsend[0] = xin_f[...]

    def fix(c, carry):
        zsend[c] = z0[c - 1] + nn(entering, (fh[c - 1], fl[c - 1]))
        return carry

    lax.fori_loop(1, NZ, fix, 0)

    def zb_copy(d):
        to = lax.rem(z + d, NZ)
        return copy(zsend.at[to], zback.at[rows_of(z)], zb_s.at[d], zb_r.at[d], zpeer(d))

    for d in order:
        zb_copy(d).start()
    zback[rows_of(z)] = zsend[z]

    for d in order:
        v_come(d).wait_recv()
        v_pass(d).start()
    v_own_come = copy(vbuf.at[z, 1 - q], vbuf.at[z, 1 - q], vo_s.at[0], vo_r.at[0], sibling)
    v_own_come.wait_recv()
    for d in order:
        v_passed(d).wait_recv()

    flows = []
    for c in range(NZ):
        found = (vbuf[c, 0, pl.ds(64, 1), pl.ds(0, H)] + vbuf[c, 1, pl.ds(64, 1), pl.ds(0, H)]).astype(jnp.int32)
        pall[:, c * H : (c + 1) * H] = one_hot(found, TOP * W)
        reach = jnp.concatenate([vbuf[c, 0, pl.ds(0, 64)], vbuf[c, 1, pl.ds(0, 64)]], axis=0)
        flows.append(nt(zsend[c], reach))
    flow_h, flow_l = split(jnp.concatenate(flows, axis=1))
    for d in order:
        copy(uy.at[pl.ds(0, Q)], zred.at[zfrom(d)], zr_s.at[d], zr_r.at[d], zpeer(d)).wait_recv()
    reduced = zred[0]
    for c in range(1, NZ):
        reduced = reduced + zred[c]
    for t in range(TOP):
        places = pall[t * W : (t + 1) * W, :]
        down = once(flow_h, places, ((1,), (1,))) + once(flow_l, places, ((1,), (1,)))
        part = jnp.where(leaf == t, reduced, 0.0) - down
        if t < 2:
            ar_a[x, t] = part
        else:
            ar_b[leaf, t - 2] = part

    def ar_copy(buf, mine, number, device):
        return copy(buf.at[mine], buf.at[mine], ar_s.at[number], ar_r.at[number], device)

    for d in range(1, NX):
        ar_copy(ar_a, x, d, xpeer(d)).start()
        ar_copy(ar_b, leaf, 4 + d, ypeer(d)).start()

    gh[NZ - 1] = ach[NZ - 1]
    gl[NZ - 1] = acl[NZ - 1]

    def suffix(i, carry):
        c = NZ - 1 - i
        gh[c], gl[c] = split(nn((ach[c], acl[c]), (gh[c + 1], gl[c + 1])))
        return carry

    lax.fori_loop(1, NZ, suffix, 0)

    for d in order:
        copy(zsend.at[0], zback.at[rows_of(zfrom(d))], zb_s.at[d], zb_r.at[d], zpeer(d)).wait_recv()
    swap_z = swap(zback, zbuf, 2)
    swap_z.start()

    for d in range(1, NX):
        ar_copy(ar_a, xfrom(d), d, xpeer(d)).wait_recv()
        ar_copy(ar_b, yfrom(d), 4 + d, ypeer(d)).wait_recv()
    ar_c[leaf] = (ar_a[0] + ar_a[1]) + (ar_a[2] + ar_a[3])
    ar_d[x] = (ar_b[0] + ar_b[1]) + (ar_b[2] + ar_b[3])
    for d in range(1, NX):
        ar_copy(ar_c, leaf, 8 + d, ypeer(d)).start()
        ar_copy(ar_d, x, 12 + d, xpeer(d)).start()

    swap_z.wait_recv()
    mine, theirs = zback[...], zbuf[...]
    entry = jnp.concatenate([jnp.where(first, mine, theirs), jnp.where(first, theirs, mine)], axis=0)
    inner = ex_r[...] + nt(entry, a0[...])
    entry = jnp.where(first, entry, inner)
    chain_inverse = split(inverse[LOC])
    bt[...] = nn(nt(rt[...] - entry, chain_inverse), chain_inverse)
    m_s[...] = jnp.where(first, bt[...], nn(bt[...], a0[...]))
    swap_m = swap(m_s, m_r, 3)
    swap_m.start()
    swap_m.wait_recv()
    bchip[...] = m_s[half] + m_r[half]

    def b_copy(d):
        to = lax.rem(z + d, NZ)
        return copy(bchip.at[rows_of(to)], bbuf.at[z], b_s.at[d], b_r.at[d], zpeer(d))

    for d in order:
        b_copy(d).start()
    bbuf[z] = bchip[rows_of(z)]

    for d in range(1, NX):
        ar_copy(ar_c, yfrom(d), 8 + d, ypeer(d)).wait_recv()
        ar_copy(ar_d, xfrom(d), 12 + d, xpeer(d)).wait_recv()
    low = (ar_c[0] + ar_c[1]) + (ar_c[2] + ar_c[3])
    high = (ar_d[0] + ar_d[1]) + (ar_d[2] + ar_d[3])
    mine_rows = pl.ds(pl.multiple_of(q * H + z * Q, Q), Q)

    sums = [low[0], low[1], high[0], high[1]]
    forward = []
    for t in range(TOP):
        value = nt(trt[t, mine_rows] - sums[t], (tih[t], til[t]))
        if t > 0:
            value = value - nt(forward[-1], (kh[t - 1], kl[t - 1]))
        forward.append(value)
    above = None
    found = [None] * TOP
    for t in reversed(range(TOP)):
        value = nn(forward[t], (tih[t], til[t]))
        if t < TOP - 1:
            value = value - nn(above, (lh[t], ll[t]))
        above = value
        found[t] = value
        topx[t] = value

    def tp_copy(d):
        return copy(topx, topt.at[:, mine_rows], tp_s.at[d], tp_r.at[d], zpeer(d))

    for d in order:
        tp_copy(d).start()
    topt[:, mine_rows] = topx[...]

    found_h, found_l = split(jnp.concatenate(found, axis=1))
    picked = once(found_h, pall[...], ((1,), (0,))) + once(found_l, pall[...], ((1,), (0,)))
    for d in order:
        copy(bchip.at[pl.ds(0, Q)], bbuf.at[zfrom(d)], b_s.at[d], b_r.at[d], zpeer(d)).wait_recv()
    for c in range(NZ):
        reach = jnp.concatenate([vbuf[c, 0, pl.ds(0, 64)], vbuf[c, 1, pl.ds(0, 64)]], axis=0)
        z0[c] = bbuf[c] - nn(picked[:, c * H : (c + 1) * H], reach)

    def back(i, carry):
        c = NZ - 1 - i
        z0[c] = z0[c] + nt(z0[c + 1], (ach[c], acl[c]))
        return carry

    lax.fori_loop(1, NZ, back, 0)

    swap_t = copy(topt.at[:, half], topt.at[:, half], up_s.at[1], up_r.at[1], sibling)
    swap_b = swap(mb_s, mb_r, 4)

    def with_top():
        for d in order:
            v_copy(d).wait_send()
            v_pass(d).wait_send()
            s_copy(d).wait_send()
            zr_copy(d).wait_send()
            zb_copy(d).wait_send()
            b_copy(d).wait_send()
        v_own.wait_send()
        for step in moves:
            for move in step:
                ring(*move).wait_send()
                ring_pass(*move).wait_send()
        for item in (swap_a, swap_s, swap_u, swap_z, swap_m):
            item.wait_send()
        for d in range(1, NX):
            y_copy(d).wait_send()
            ar_copy(ar_a, x, d, xpeer(d)).wait_send()
            ar_copy(ar_b, leaf, 4 + d, ypeer(d)).wait_send()
            ar_copy(ar_c, leaf, 8 + d, ypeer(d)).wait_send()
            ar_copy(ar_d, x, 12 + d, xpeer(d)).wait_send()

        @pl.when(x < NX - 1)
        def _():
            hop_f.wait_send()

        for d in order:
            place = pl.ds(pl.multiple_of(q * H + zfrom(d) * Q, Q), Q)
            copy(topx, topt.at[:, place], tp_s.at[d], tp_r.at[d], zpeer(d)).wait_recv()
        swap_t.start()
        copy(topt.at[:, other], topt.at[:, other], up_s.at[1], up_r.at[1], sibling).wait_recv()
        pick, pick_chain = 0.0, 0.0
        for t in range(TOP):
            here = pl.ds(t * W, W)
            value = topt[t].T
            top_out[t] = value
            vh, vl = split(value)
            near, far = pt[pl.ds(0, 512), here], pt[pl.ds(512, 64), here]
            pick = pick + (once(near, vh, ((1,), (0,))) + once(near, vl, ((1,), (0,))))
            pick_chain = pick_chain + (once(far, vh, ((1,), (0,))) + once(far, vl, ((1,), (0,))))
        ycat[...] = pick
        bt[...] = bt[...] - tn(pick_chain, side_v[...])
        mb_s[...] = nn(bt[...], a0[...])
        swap_b.start()

        def lower(k):
            hval[k] = hval[k] - tn((n1h[k], n1l[k]), ycat[pl.ds(pl.multiple_of(k * 64, 64), 64)])

        by_four(lower)

    @pl.when(x == 0)
    def _():
        with_top()

    hop_b = copy(xout_b, xin_b, xb_s.at[0], xb_r.at[0], at(lax.rem(x + NX - 1, NX), z, q))

    @pl.when(x == NX - 1)
    def _():
        xin_b[...] = jnp.zeros((Q, W), F32)
        xout_b[...] = z0[0]

    @pl.when(x < NX - 1)
    def _():
        hop_b.wait_recv()
        xout_b[...] = z0[0] + nt(xin_b[...], (fh[NZ - 1], fl[NZ - 1]))

    @pl.when(x > 0)
    def _():
        hop_b.start()

    leaving = split(xin_b[...])
    xsend[NZ - 1] = xin_b[...]

    def unfix(c, carry):
        xsend[c] = z0[c + 1] + nt(leaving, (gh[c + 1], gl[c + 1]))
        return carry

    lax.fori_loop(0, NZ - 1, unfix, 0)

    def xa_copy(d):
        to = lax.rem(z + d, NZ)
        return copy(xsend.at[to], xback.at[rows_of(z)], xa_s.at[d], xa_r.at[d], zpeer(d))

    for d in order:
        xa_copy(d).start()
    xback[rows_of(z)] = xsend[z]

    @pl.when(x > 0)
    def _():
        with_top()

    top_store = pltpu.make_async_copy(top_out, top_to, store.at[LOC + 1])
    top_store.start()
    swap_b.wait_recv()
    base = bt[...] + jnp.where(first, mb_r[...], 0.0)
    for d in order:
        copy(xsend.at[0], xback.at[rows_of(zfrom(d))], xa_s.at[d], xa_r.at[d], zpeer(d)).wait_recv()
    swap_x = swap(xback, zbuf, 5)
    swap_x.start()
    swap_x.wait_recv()
    mine, theirs = xback[...], zbuf[...]
    exits = jnp.concatenate([jnp.where(first, mine, theirs), jnp.where(first, theirs, mine)], axis=0)
    out[LOC] = (base + nn(exits, msel[...])).T

    def keep(k):
        return pltpu.make_async_copy(out.at[k], out_to.at[k], store.at[k])

    keep(LOC).start()
    for k in reversed(range(LOC)):
        out[k] = hval[k] - tn((dh[k], dl[k]), out[links[0, k]])
        keep(k).start()
    for k in range(LOC + 1):
        keep(k).wait()
    top_store.wait()

    for d in order:
        tp_copy(d).wait_send()
        xa_copy(d).wait_send()
    for item in (swap_t, swap_b, swap_x):
        item.wait_send()

    @pl.when(x > 0)
    def _():
        hop_b.wait_send()


def shards(
    node_rhs, node_inverse, local_blocks, chain_next, chain_top, top_rhs, top_inverse, top_next,
    ancestors, block_rows, chain_target, chain_rows,
):
    vmem = pl.BlockSpec(memory_space=pltpu.VMEM)
    smem = pl.BlockSpec(memory_space=pltpu.SMEM)
    hbm = pl.BlockSpec(memory_space=pl.ANY)

    def f32(*shape):
        return pltpu.VMEM(shape, F32)

    def b16(*shape):
        return pltpu.VMEM(shape, BF16)

    def sem(count):
        return pltpu.SemaphoreType.DMA((count,))

    scratch = [
        f32(LOC + 1, W, W), f32(LOC + 1, W, W), f32(LOC, 128, W), f32(TOP, W, W), f32(TOP, W, W),
        f32(TOP - 1, W, W), f32(LOC + 1, W, W), f32(TOP, W, W),
        b16(LOC, W, W), b16(LOC, W, W), b16(LOC, 64, W), b16(LOC, 64, W), f32(512, W), b16(576, TOP * W),
        f32(LOC, W, W), f32(TOP, W, W), f32(TOP, H, W), f32(TOP, H, W), f32(NY, H, W), f32(H, W), f32(NZ, Q, W),
        f32(W, W), f32(W, W), f32(W, W), f32(W, W), f32(W, W), f32(64, W),
        f32(NZ, W, W), b16(NZ, W, W), b16(NZ, W, W), b16(NZ, W, W), b16(NZ, W, W), b16(NZ, W, W), b16(NZ, W, W),
        f32(NZ, 2, 72, W), b16(TOP * W, NZ * H),
        f32(W, W), f32(W, W), f32(W, W), f32(H, W), f32(NZ, Q, W), f32(NZ, Q, W), f32(NZ, Q, W), f32(H, W),
        f32(H, W), f32(Q, W), f32(Q, W),
        f32(NX, 2, Q, W), f32(NY, 2, Q, W), f32(NY, 2, Q, W), f32(NX, 2, Q, W),
        f32(TOP, Q, W), f32(TOP, W, W), f32(TOP, W, W), b16(TOP, W, W), b16(TOP, W, W),
        b16(TOP - 1, W, W), b16(TOP - 1, W, W), b16(TOP - 1, W, W), b16(TOP - 1, W, W),
        f32(W, W), f32(W, W), f32(W, W), f32(H, W), f32(NZ, Q, W), f32(NZ, Q, W), f32(H, W),
        f32(Q, W), f32(Q, W), f32(W, W), f32(W, W),
        sem(7), sem(LOC + 2), sem(6), sem(6), sem(16), sem(16), sem(16), sem(16), sem(8), sem(8), sem(8), sem(8),
        sem(1), sem(1),
        sem(8), sem(8), sem(2), sem(2), sem(4), sem(4), sem(8), sem(8), sem(1), sem(1), sem(8), sem(8),
        sem(16), sem(16), sem(8), sem(8), sem(1), sem(1), sem(8), sem(8), sem(8), sem(8),
    ]
    solved, top = pl.pallas_call(
        kernel,
        out_shape=(
            jax.ShapeDtypeStruct((LOC + 1, W, W), F32),
            jax.ShapeDtypeStruct((TOP, W, W), F32),
        ),
        in_specs=[smem, smem, hbm, hbm, hbm, vmem, vmem, hbm, hbm, hbm, vmem, vmem],
        out_specs=(hbm, hbm),
        scratch_shapes=scratch,
        compiler_params=pltpu.CompilerParams(
            collective_id=0, has_side_effects=True, vmem_limit_bytes=56 * 1024 * 1024
        ),
    )(
        ancestors[0, 0].T,
        chain_target[0],
        node_rhs[0, 0],
        node_inverse[0, 0],
        local_blocks[0, 0].reshape(LOC, 128, W),
        chain_next[0, 0],
        chain_top[0, 0],
        top_rhs,
        top_inverse,
        top_next,
        block_rows[0, 0].reshape(2 * LOC, 64),
        chain_rows[0],
    )
    return solved[None, None], top


def solution(mesh):
    placed = (
        P("leaf", "col", None, None, None),
        P("leaf", "col", None, None, None),
        P("leaf", "col", None, None, None, None),
        P("leaf", "col", None, None),
        P("leaf", "col", None, None),
        P(),
        P(),
        P(),
        P("leaf", "col", None, None),
        P("leaf", "col", None, None, None),
        P("leaf", "col"),
        P("leaf", "col", None),
    )
    return jax.shard_map(
        shards,
        mesh=mesh,
        in_specs=placed,
        out_specs=(P("leaf", "col", None, None, None), P()),
        check_vma=False,
    )
```

```python
import jax
import jax.numpy as jnp
from jax import lax
from jax.experimental import pallas as pl
from jax.experimental.pallas import tpu as pltpu
from jax.sharding import PartitionSpec as P

F32 = jnp.float32
BF16 = jnp.bfloat16
MESH = pl.DeviceIdType.MESH
NX, NZ, NY, NCOL = 4, 8, 4, 64
W = 256
H = 128
Q = 16
LOC = 8
TOP = 4


def split(value):
    if isinstance(value, tuple):
        return value
    high = value.astype(BF16)
    return high, (value - high.astype(F32)).astype(BF16)


def once(left, right, dims):
    return lax.dot_general(left, right, (dims, ((), ())), preferred_element_type=F32)


def thrice(left, right, dims):
    lh, ll = split(left)
    rh, rl = split(right)
    return once(lh, rh, dims) + (once(lh, rl, dims) + once(ll, rh, dims))


def nn(left, right):
    return thrice(left, right, ((1,), (0,)))


def nt(left, right):
    return thrice(left, right, ((1,), (1,)))


def tn(left, right):
    return thrice(left, right, ((0,), (0,)))


def one_hot(index_row, extent):
    place = lax.broadcasted_iota(jnp.int32, (extent, index_row.shape[1]), 0)
    return jnp.where(place == index_row, 1.0, 0.0).astype(BF16)


def kernel(
    links, target, rhs_in, inverse_in, blocks_in, onward, sideways, top_rhs_in, top_inverse_in, top_next_in, rows, chain_rows,
    out_to, top_to,
    src, inverse, blocks, top_rhs, top_inverse, top_next, out, top_out,
    dh, dl, n1h, n1l, ycat, pt, hval, upt, uprecv, uph, ybuf, uy, zred,
    a_own, a_sib, a0, a1, msel, side_v, acf, ach, acl, fh, fl, gh, gl, vbuf, pall,
    rt, ex_s, ex_r, schip, sbuf, z0, zsend, zbuf, zback, xin_f, xout_f,
    ar_a, ar_b, ar_c, ar_d, topx, topt, trt, tih, til, kh, kl, lh, ll,
    bt, m_s, m_r, bchip, bbuf, xsend, xback, xin_b, xout_b, mb_s, mb_r,
    load, store, core_s, core_r, ac_s, ac_r, acx_s, acx_r, v_s, v_r, vx_s, vx_r, vo_s, vo_r,
    s_s, s_r, up_s, up_r, y_s, y_r, zr_s, zr_r, xf_s, xf_r, zb_s, zb_r, ar_s, ar_r,
    b_s, b_r, xb_s, xb_r, xa_s, xa_r, tp_s, tp_r,
):
    leaf = lax.axis_index("leaf")
    col = lax.axis_index("col")
    x, z, q = col // 16, (col // 2) % NZ, col % 2

    def at(xx, zz, qq):
        return (leaf, xx * 16 + zz * 2 + qq)

    sibling = at(x, z, 1 - q)

    def zpeer(d):
        return at(x, lax.rem(z + d, NZ), q)

    def xpeer(d):
        return at(lax.rem(x + d, NX), z, q)

    def ypeer(d):
        return (lax.rem(leaf + d, NY), col)

    def zfrom(d):
        return lax.rem(z + NZ - d, NZ)

    def xfrom(d):
        return lax.rem(x + NX - d, NX)

    def yfrom(d):
        return lax.rem(leaf + NY - d, NY)

    def copy(source, goal, ss, rs, device):
        return pltpu.make_async_remote_copy(
            src_ref=source, dst_ref=goal, send_sem=ss, recv_sem=rs, device_id=device, device_id_type=MESH
        )

    def swap(source, goal, number):
        return copy(source, goal, core_s.at[number], core_r.at[number], sibling)

    barrier = pltpu.get_barrier_semaphore()
    peers = [sibling] + [zpeer(d) for d in range(1, NZ)] + [xpeer(d) for d in range(1, NX)]
    peers = peers + [ypeer(d) for d in range(1, NY)]
    for peer in peers:
        pl.semaphore_signal(barrier, inc=1, device_id=peer, device_id_type=MESH)

    loads = [
        pltpu.make_async_copy(inverse_in.at[LOC], inverse.at[LOC], load.at[0]),
        pltpu.make_async_copy(inverse_in.at[pl.ds(0, LOC)], inverse.at[pl.ds(0, LOC)], load.at[1]),
        pltpu.make_async_copy(blocks_in, blocks, load.at[2]),
        pltpu.make_async_copy(rhs_in, src, load.at[3]),
        pltpu.make_async_copy(top_inverse_in, top_inverse, load.at[4]),
        pltpu.make_async_copy(top_next_in, top_next, load.at[5]),
        pltpu.make_async_copy(top_rhs_in, top_rhs, load.at[6]),
    ]
    for item in loads:
        item.start()

    first = q == 0
    half = pl.ds(pl.multiple_of(q * H, H), H)
    other = pl.ds(pl.multiple_of((1 - q) * H, H), H)

    def rows_of(zz):
        return pl.ds(pl.multiple_of(zz * Q, Q), Q)

    def by_four(body):
        def four(i, carry):
            for j in range(4):
                body(4 * i + j)
            return carry

        lax.fori_loop(0, 2, four, 0)

    loads[0].wait()
    chain_inverse = split(inverse[LOC])
    coupling = jnp.where(col == NCOL - 1, jnp.zeros((W, W), F32), onward[...])
    a_own[...] = -nn(coupling, chain_inverse)
    pl.semaphore_wait(barrier, len(peers))
    swap_a = swap(a_own, a_sib, 0)
    swap_a.start()
    side = nn(sideways[...], chain_inverse)
    side_v[...] = side
    loads[1].wait()
    loads[2].wait()

    def local_map(k):
        near = nn(blocks[k], inverse[k])
        near_h, near_l = split(near)
        to_parent = one_hot(rows[pl.ds(2 * k, 1), :], W)
        dh[k] = once(to_parent, near_h[:64], ((1,), (0,))).astype(BF16)
        dl[k] = once(to_parent, near_l[:64], ((1,), (0,))).astype(BF16)
        n1h[k] = near_h[64:]
        n1l[k] = near_l[64:]

    def some_maps(start):
        def two(i, carry):
            local_map(start + 2 * i)
            local_map(start + 2 * i + 1)
            return carry

        lax.fori_loop(0, 2, two, 0)

    swap_a.wait_recv()
    a0[...] = jnp.where(first, a_own[...], a_sib[...])
    a1[...] = jnp.where(first, a_sib[...], a_own[...])
    pair = nn(a1[...], a0[...])
    acf[z] = pair.T

    def ring_part(core, way, s, h):
        slot = lax.rem(z + NZ - s * way, NZ)
        return acf.at[slot, pl.ds(pl.multiple_of(core * H + h * 64, 64), 64)]

    def ring_number(way, s, h):
        return ((way + 1) // 2 * 4 + s) * 2 + h

    def ring(way, s, h):
        part, i = ring_part(q, way, s, h), ring_number(way, s, h)
        return copy(part, part, ac_s.at[i], ac_r.at[i], zpeer(way % NZ))

    def ring_in(way, s, h):
        part, i = ring_part(q, way, s + 1, h), ring_number(way, s, h)
        return copy(part, part, ac_s.at[i], ac_r.at[i], zpeer(way % NZ))

    def ring_pass(way, s, h):
        part, i = ring_part(q, way, s + 1, h), ring_number(way, s, h)
        return copy(part, part, acx_s.at[i], acx_r.at[i], sibling)

    def ring_passed(way, s, h):
        part, i = ring_part(1 - q, way, s + 1, h), ring_number(way, s, h)
        return copy(part, part, acx_s.at[i], acx_r.at[i], sibling)

    moves = [[(way, s, h) for h in range(2) for way in (1, -1)] for s in range(3)]
    moves.append([(1, 3, 0), (-1, 3, 1)])

    def ring_step(s):
        if s > 0:
            for way, _, h in moves[s - 1]:
                ring_in(way, s - 1, h).wait_recv()
                if s < 4 and (way, s, h) in moves[s]:
                    ring(way, s, h).start()
                ring_pass(way, s - 1, h).start()
        else:
            for way, _, h in moves[0]:
                ring(way, 0, h).start()

    ring_step(0)
    msel[...] = jnp.where(first, pair, a_own[...])
    vbuf[z, q, pl.ds(0, 64)] = jnp.where(first, side, nn(side, a0[...]))
    index = (chain_rows[...] + target[0] * W).astype(F32)
    empty = jnp.zeros((1, 64), F32)
    index = jnp.concatenate(
        [jnp.where(first, index, empty), jnp.where(first, empty, index), jnp.zeros((1, 128), F32)], axis=1
    )
    vbuf[z, q, pl.ds(64, 8)] = jnp.broadcast_to(index, (8, W))

    def v_copy(d):
        return copy(vbuf.at[z, q], vbuf.at[z, q], v_s.at[d], v_r.at[d], zpeer(d))

    order = (1, 7, 2, 6, 3, 5, 4)
    direct = (5, 3, 2, 6, 1, 7)
    v_own = copy(vbuf.at[z, q], vbuf.at[z, q], vo_s.at[0], vo_r.at[0], sibling)
    v_own.start()
    some_maps(0)
    ring_step(1)
    some_maps(4)
    ring_step(2)
    loads[3].wait()

    for k in range(LOC):
        update = nn((dh[k], dl[k]), src[k])
        for j in range(k + 1, LOC + 1):
            src[j] = src[j] - jnp.where(links[0, k] == j, update, 0.0)

    ring_step(3)
    rt[...] = src[LOC].T
    ex_s[...] = jnp.where(first, -nt(rt[...], a_own[...]), rt[...])
    swap_s = swap(ex_s, ex_r, 1)
    swap_s.start()
    swap_s.wait_recv()
    shift_half = jnp.where(first, ex_s[half], ex_r[half])
    rest_half = jnp.where(first, ex_r[half], ex_s[half])
    schip[...] = -nt(rest_half - shift_half, a1[...])

    def s_copy(d):
        to = lax.rem(z + d, NZ)
        return copy(schip.at[rows_of(to)], sbuf.at[z], s_s.at[d], s_r.at[d], zpeer(d))

    for d in order:
        s_copy(d).start()
    sbuf[z] = schip[rows_of(z)]

    for d in direct:
        v_copy(d).start()

    ring_step(4)

    def up_part(k):
        ycat[pl.ds(pl.multiple_of(k * 64, 64), 64)] = nn((n1h[k], n1l[k]), src[k])

    by_four(up_part)
    diagonal = lax.broadcasted_iota(jnp.int32, (64, 64), 0) == lax.broadcasted_iota(jnp.int32, (64, 64), 1)

    def places_of(index_row):
        column = jnp.sum(jnp.where(diagonal, index_row, 0.0), axis=1, keepdims=True).astype(jnp.int32)
        place = lax.broadcasted_iota(jnp.int32, (64, TOP * W), 1)
        return jnp.where(place == column, 1.0, 0.0).astype(BF16)

    def places_body(k):
        index_row = (rows[pl.ds(2 * k + 1, 1), :] + links[1, k] * W).astype(F32)
        pt[pl.ds(pl.multiple_of(k * 64, 64), 64)] = places_of(index_row)

    by_four(places_body)
    pt[pl.ds(512, 64)] = places_of((chain_rows[...] + target[0] * W).astype(F32))
    up_h, up_l = split(ycat[...].T)
    chain_h, chain_l = split(nt(jnp.where(first, rt[...], rt[...] - ex_r[...]), side_v[...]))
    for t in range(TOP):
        here = pl.ds(t * W, W)
        near, far = pt[pl.ds(0, 512), here], pt[pl.ds(512, 64), here]
        near = once(up_h, near, ((1,), (0,))) + once(up_l, near, ((1,), (0,)))
        far = once(chain_h, far, ((1,), (0,))) + once(chain_l, far, ((1,), (0,)))
        upt[t] = near + far
    swap_u = copy(upt.at[:, other], uprecv, up_s.at[0], up_r.at[0], sibling)
    swap_u.start()

    for item in loads[4:]:
        item.wait()
    for t in range(TOP):
        th, tl = split(top_inverse[t])
        tih[t] = th
        til[t] = tl
        trt[t] = top_rhs[t].T
    for t in range(TOP - 1):
        kh[t], kl[t] = split(nn((tih[t + 1], til[t + 1]), top_next[t]))
        lh[t], ll[t] = split(nn(top_next[t], (tih[t], til[t])))
    swap_u.wait_recv()
    for t in range(TOP):
        uph[t] = upt[t, half] + uprecv[t]

    def y_copy(d):
        return copy(uph.at[lax.rem(leaf + d, NY)], ybuf.at[leaf], y_s.at[d], y_r.at[d], ypeer(d))

    for d in range(1, NY):
        y_copy(d).start()
    ybuf[leaf] = uph[leaf]

    def square(k):
        here = split(inverse[k])
        hval[k] = tn(here, nn(here, src[k]))

    def v_come(d):
        part = vbuf.at[zfrom(d), q]
        return copy(part, part, v_s.at[d], v_r.at[d], zpeer(d))

    def v_pass(d):
        part = vbuf.at[zfrom(d), q]
        return copy(part, part, vx_s.at[d], vx_r.at[d], sibling)

    def v_passed(d):
        part = vbuf.at[zfrom(d), 1 - q]
        return copy(part, part, vx_s.at[d], vx_r.at[d], sibling)

    for step in moves:
        for move in step:
            ring_passed(*move).wait_recv()

    def halves(c, carry):
        ach[c], acl[c] = split(acf[c])
        return carry

    lax.fori_loop(0, NZ, halves, 0)
    for d in order:
        copy(schip.at[pl.ds(0, Q)], sbuf.at[zfrom(d)], s_s.at[d], s_r.at[d], zpeer(d)).wait_recv()

    z0[0] = sbuf[0]
    fh[0] = ach[0]
    fl[0] = acl[0]

    def prefix(c, carry):
        here = (ach[c], acl[c])
        z0[c] = sbuf[c] + nn(z0[c - 1], here)
        fh[c], fl[c] = split(nn((fh[c - 1], fl[c - 1]), here))
        return carry

    lax.fori_loop(1, NZ, prefix, 0)

    v_come(5).wait_recv()
    third = vbuf.at[zfrom(5), q]
    copy(third, third, v_s.at[4], v_r.at[4], zpeer(7)).start()
    v_pass(5).start()

    @pl.when(x >= 2)
    def _():
        by_four(square)

    whole = (fh[NZ - 1], fl[NZ - 1])
    hop_f = copy(xout_f, xin_f, xf_s.at[0], xf_r.at[0], at(lax.rem(x + 1, NX), z, q))

    @pl.when(x == 0)
    def _():
        xin_f[...] = jnp.zeros((Q, W), F32)
        xout_f[...] = z0[NZ - 1]

    @pl.when(x > 0)
    def _():
        hop_f.wait_recv()
        xout_f[...] = z0[NZ - 1] + nn(xin_f[...], whole)

    @pl.when(x < NX - 1)
    def _():
        hop_f.start()

    for d in range(1, NY):
        copy(uph.at[0], ybuf.at[yfrom(d)], y_s.at[d], y_r.at[d], ypeer(d)).wait_recv()
    uy[...] = (ybuf[0] + ybuf[1]) + (ybuf[2] + ybuf[3])

    def zr_copy(d):
        to = lax.rem(z + d, NZ)
        return copy(uy.at[rows_of(to)], zred.at[z], zr_s.at[d], zr_r.at[d], zpeer(d))

    for d in order:
        zr_copy(d).start()
    zred[z] = uy[rows_of(z)]

    @pl.when(x < 2)
    def _():
        by_four(square)

    entering = split(xin_f[...])
    zsend[0] = xin_f[...]

    def fix(c, carry):
        zsend[c] = z0[c - 1] + nn(entering, (fh[c - 1], fl[c - 1]))
        return carry

    lax.fori_loop(1, NZ, fix, 0)

    def zb_copy(d):
        to = lax.rem(z + d, NZ)
        return copy(zsend.at[to], zback.at[rows_of(z)], zb_s.at[d], zb_r.at[d], zpeer(d))

    for d in order:
        zb_copy(d).start()
    zback[rows_of(z)] = zsend[z]

    for d in (3, 2, 6, 1, 7, 4):
        v_come(d).wait_recv()
        v_pass(d).start()
    v_own_come = copy(vbuf.at[z, 1 - q], vbuf.at[z, 1 - q], vo_s.at[0], vo_r.at[0], sibling)
    v_own_come.wait_recv()
    for d in order:
        v_passed(d).wait_recv()

    flows = []
    for c in range(NZ):
        found = (vbuf[c, 0, pl.ds(64, 1), pl.ds(0, H)] + vbuf[c, 1, pl.ds(64, 1), pl.ds(0, H)]).astype(jnp.int32)
        pall[:, c * H : (c + 1) * H] = one_hot(found, TOP * W)
        reach = jnp.concatenate([vbuf[c, 0, pl.ds(0, 64)], vbuf[c, 1, pl.ds(0, 64)]], axis=0)
        flows.append(nt(zsend[c], reach))
    flow_h, flow_l = split(jnp.concatenate(flows, axis=1))
    for d in order:
        copy(uy.at[pl.ds(0, Q)], zred.at[zfrom(d)], zr_s.at[d], zr_r.at[d], zpeer(d)).wait_recv()
    reduced = zred[0]
    for c in range(1, NZ):
        reduced = reduced + zred[c]
    for t in range(TOP):
        places = pall[t * W : (t + 1) * W, :]
        down = once(flow_h, places, ((1,), (1,))) + once(flow_l, places, ((1,), (1,)))
        part = jnp.where(leaf == t, reduced, 0.0) - down
        if t < 2:
            ar_a[x, t] = part
        else:
            ar_b[leaf, t - 2] = part

    def ar_copy(buf, mine, number, device):
        return copy(buf.at[mine], buf.at[mine], ar_s.at[number], ar_r.at[number], device)

    for d in range(1, NX):
        ar_copy(ar_a, x, d, xpeer(d)).start()
        ar_copy(ar_b, leaf, 4 + d, ypeer(d)).start()

    gh[NZ - 1] = ach[NZ - 1]
    gl[NZ - 1] = acl[NZ - 1]

    def suffix(i, carry):
        c = NZ - 1 - i
        gh[c], gl[c] = split(nn((ach[c], acl[c]), (gh[c + 1], gl[c + 1])))
        return carry

    lax.fori_loop(1, NZ, suffix, 0)

    for d in order:
        copy(zsend.at[0], zback.at[rows_of(zfrom(d))], zb_s.at[d], zb_r.at[d], zpeer(d)).wait_recv()
    swap_z = swap(zback, zbuf, 2)
    swap_z.start()

    for d in range(1, NX):
        ar_copy(ar_a, xfrom(d), d, xpeer(d)).wait_recv()
        ar_copy(ar_b, yfrom(d), 4 + d, ypeer(d)).wait_recv()
    ar_c[leaf] = (ar_a[0] + ar_a[1]) + (ar_a[2] + ar_a[3])
    ar_d[x] = (ar_b[0] + ar_b[1]) + (ar_b[2] + ar_b[3])
    for d in range(1, NX):
        ar_copy(ar_c, leaf, 8 + d, ypeer(d)).start()
        ar_copy(ar_d, x, 12 + d, xpeer(d)).start()

    swap_z.wait_recv()
    mine, theirs = zback[...], zbuf[...]
    entry = jnp.concatenate([jnp.where(first, mine, theirs), jnp.where(first, theirs, mine)], axis=0)
    inner = ex_r[...] + nt(entry, a0[...])
    entry = jnp.where(first, entry, inner)
    chain_inverse = split(inverse[LOC])
    bt[...] = nn(nt(rt[...] - entry, chain_inverse), chain_inverse)
    m_s[...] = jnp.where(first, bt[...], nn(bt[...], a0[...]))
    swap_m = swap(m_s, m_r, 3)
    swap_m.start()
    swap_m.wait_recv()
    bchip[...] = m_s[half] + m_r[half]

    def b_copy(d):
        to = lax.rem(z + d, NZ)
        return copy(bchip.at[rows_of(to)], bbuf.at[z], b_s.at[d], b_r.at[d], zpeer(d))

    for d in order:
        b_copy(d).start()
    bbuf[z] = bchip[rows_of(z)]

    for d in range(1, NX):
        ar_copy(ar_c, yfrom(d), 8 + d, ypeer(d)).wait_recv()
        ar_copy(ar_d, xfrom(d), 12 + d, xpeer(d)).wait_recv()
    low = (ar_c[0] + ar_c[1]) + (ar_c[2] + ar_c[3])
    high = (ar_d[0] + ar_d[1]) + (ar_d[2] + ar_d[3])
    mine_rows = pl.ds(pl.multiple_of(q * H + z * Q, Q), Q)

    sums = [low[0], low[1], high[0], high[1]]
    forward = []
    for t in range(TOP):
        value = nt(trt[t, mine_rows] - sums[t], (tih[t], til[t]))
        if t > 0:
            value = value - nt(forward[-1], (kh[t - 1], kl[t - 1]))
        forward.append(value)
    above = None
    found = [None] * TOP
    for t in reversed(range(TOP)):
        value = nn(forward[t], (tih[t], til[t]))
        if t < TOP - 1:
            value = value - nn(above, (lh[t], ll[t]))
        above = value
        found[t] = value
        topx[t] = value

    def tp_copy(d):
        return copy(topx, topt.at[:, mine_rows], tp_s.at[d], tp_r.at[d], zpeer(d))

    for d in direct:
        tp_copy(d).start()
    topt[:, mine_rows] = topx[...]

    found_h, found_l = split(jnp.concatenate(found, axis=1))
    picked = once(found_h, pall[...], ((1,), (0,))) + once(found_l, pall[...], ((1,), (0,)))
    for d in order:
        copy(bchip.at[pl.ds(0, Q)], bbuf.at[zfrom(d)], b_s.at[d], b_r.at[d], zpeer(d)).wait_recv()
    for c in range(NZ):
        reach = jnp.concatenate([vbuf[c, 0, pl.ds(0, 64)], vbuf[c, 1, pl.ds(0, 64)]], axis=0)
        z0[c] = bbuf[c] - nn(picked[:, c * H : (c + 1) * H], reach)

    def back(i, carry):
        c = NZ - 1 - i
        z0[c] = z0[c] + nt(z0[c + 1], (ach[c], acl[c]))
        return carry

    lax.fori_loop(1, NZ, back, 0)

    swap_t = copy(topt.at[:, half], topt.at[:, half], up_s.at[1], up_r.at[1], sibling)
    swap_b = swap(mb_s, mb_r, 4)

    def with_top():
        def top_come(d):
            place = pl.ds(pl.multiple_of(q * H + zfrom(d) * Q, Q), Q)
            return copy(topx, topt.at[:, place], tp_s.at[d], tp_r.at[d], zpeer(d))

        top_come(5).wait_recv()
        third = topt.at[:, pl.ds(pl.multiple_of(q * H + zfrom(5) * Q, Q), Q)]
        copy(third, third, tp_s.at[4], tp_r.at[4], zpeer(7)).start()
        for d in order:
            v_copy(d).wait_send()
            v_pass(d).wait_send()
            s_copy(d).wait_send()
            zr_copy(d).wait_send()
            zb_copy(d).wait_send()
            b_copy(d).wait_send()
        v_own.wait_send()
        for step in moves:
            for move in step:
                ring(*move).wait_send()
                ring_pass(*move).wait_send()
        for item in (swap_a, swap_s, swap_u, swap_z, swap_m):
            item.wait_send()
        for d in range(1, NX):
            y_copy(d).wait_send()
            ar_copy(ar_a, x, d, xpeer(d)).wait_send()
            ar_copy(ar_b, leaf, 4 + d, ypeer(d)).wait_send()
            ar_copy(ar_c, leaf, 8 + d, ypeer(d)).wait_send()
            ar_copy(ar_d, x, 12 + d, xpeer(d)).wait_send()

        @pl.when(x < NX - 1)
        def _():
            hop_f.wait_send()

        for d in (3, 2, 6, 1, 7, 4):
            top_come(d).wait_recv()
        swap_t.start()
        copy(topt.at[:, other], topt.at[:, other], up_s.at[1], up_r.at[1], sibling).wait_recv()
        pick, pick_chain = 0.0, 0.0
        for t in range(TOP):
            here = pl.ds(t * W, W)
            value = topt[t].T
            top_out[t] = value
            vh, vl = split(value)
            near, far = pt[pl.ds(0, 512), here], pt[pl.ds(512, 64), here]
            pick = pick + (once(near, vh, ((1,), (0,))) + once(near, vl, ((1,), (0,))))
            pick_chain = pick_chain + (once(far, vh, ((1,), (0,))) + once(far, vl, ((1,), (0,))))
        ycat[...] = pick
        bt[...] = bt[...] - tn(pick_chain, side_v[...])
        mb_s[...] = nn(bt[...], a0[...])
        swap_b.start()

        def lower(k):
            hval[k] = hval[k] - tn((n1h[k], n1l[k]), ycat[pl.ds(pl.multiple_of(k * 64, 64), 64)])

        by_four(lower)

    @pl.when(x == 0)
    def _():
        with_top()

    hop_b = copy(xout_b, xin_b, xb_s.at[0], xb_r.at[0], at(lax.rem(x + NX - 1, NX), z, q))

    @pl.when(x == NX - 1)
    def _():
        xin_b[...] = jnp.zeros((Q, W), F32)
        xout_b[...] = z0[0]

    @pl.when(x < NX - 1)
    def _():
        hop_b.wait_recv()
        xout_b[...] = z0[0] + nt(xin_b[...], (fh[NZ - 1], fl[NZ - 1]))

    @pl.when(x > 0)
    def _():
        hop_b.start()

    leaving = split(xin_b[...])
    xsend[NZ - 1] = xin_b[...]

    def unfix(c, carry):
        xsend[c] = z0[c + 1] + nt(leaving, (gh[c + 1], gl[c + 1]))
        return carry

    lax.fori_loop(0, NZ - 1, unfix, 0)

    def xa_copy(d):
        to = lax.rem(z + d, NZ)
        return copy(xsend.at[to], xback.at[rows_of(z)], xa_s.at[d], xa_r.at[d], zpeer(d))

    for d in order:
        xa_copy(d).start()
    xback[rows_of(z)] = xsend[z]

    @pl.when(x > 0)
    def _():
        with_top()

    top_store = pltpu.make_async_copy(top_out, top_to, store.at[LOC + 1])
    top_store.start()
    swap_b.wait_recv()
    base = bt[...] + jnp.where(first, mb_r[...], 0.0)
    for d in order:
        copy(xsend.at[0], xback.at[rows_of(zfrom(d))], xa_s.at[d], xa_r.at[d], zpeer(d)).wait_recv()
    swap_x = swap(xback, zbuf, 5)
    swap_x.start()
    swap_x.wait_recv()
    mine, theirs = xback[...], zbuf[...]
    exits = jnp.concatenate([jnp.where(first, mine, theirs), jnp.where(first, theirs, mine)], axis=0)
    out[LOC] = (base + nn(exits, msel[...])).T

    def keep(k):
        return pltpu.make_async_copy(out.at[k], out_to.at[k], store.at[k])

    keep(LOC).start()
    for k in reversed(range(LOC)):
        out[k] = hval[k] - tn((dh[k], dl[k]), out[links[0, k]])
        keep(k).start()
    for k in range(LOC + 1):
        keep(k).wait()
    top_store.wait()

    for d in order:
        tp_copy(d).wait_send()
        xa_copy(d).wait_send()
    for item in (swap_t, swap_b, swap_x):
        item.wait_send()

    @pl.when(x > 0)
    def _():
        hop_b.wait_send()


def shards(
    node_rhs, node_inverse, local_blocks, chain_next, chain_top, top_rhs, top_inverse, top_next,
    ancestors, block_rows, chain_target, chain_rows,
):
    vmem = pl.BlockSpec(memory_space=pltpu.VMEM)
    smem = pl.BlockSpec(memory_space=pltpu.SMEM)
    hbm = pl.BlockSpec(memory_space=pl.ANY)

    def f32(*shape):
        return pltpu.VMEM(shape, F32)

    def b16(*shape):
        return pltpu.VMEM(shape, BF16)

    def sem(count):
        return pltpu.SemaphoreType.DMA((count,))

    scratch = [
        f32(LOC + 1, W, W), f32(LOC + 1, W, W), f32(LOC, 128, W), f32(TOP, W, W), f32(TOP, W, W),
        f32(TOP - 1, W, W), f32(LOC + 1, W, W), f32(TOP, W, W),
        b16(LOC, W, W), b16(LOC, W, W), b16(LOC, 64, W), b16(LOC, 64, W), f32(512, W), b16(576, TOP * W),
        f32(LOC, W, W), f32(TOP, W, W), f32(TOP, H, W), f32(TOP, H, W), f32(NY, H, W), f32(H, W), f32(NZ, Q, W),
        f32(W, W), f32(W, W), f32(W, W), f32(W, W), f32(W, W), f32(64, W),
        f32(NZ, W, W), b16(NZ, W, W), b16(NZ, W, W), b16(NZ, W, W), b16(NZ, W, W), b16(NZ, W, W), b16(NZ, W, W),
        f32(NZ, 2, 72, W), b16(TOP * W, NZ * H),
        f32(W, W), f32(W, W), f32(W, W), f32(H, W), f32(NZ, Q, W), f32(NZ, Q, W), f32(NZ, Q, W), f32(H, W),
        f32(H, W), f32(Q, W), f32(Q, W),
        f32(NX, 2, Q, W), f32(NY, 2, Q, W), f32(NY, 2, Q, W), f32(NX, 2, Q, W),
        f32(TOP, Q, W), f32(TOP, W, W), f32(TOP, W, W), b16(TOP, W, W), b16(TOP, W, W),
        b16(TOP - 1, W, W), b16(TOP - 1, W, W), b16(TOP - 1, W, W), b16(TOP - 1, W, W),
        f32(W, W), f32(W, W), f32(W, W), f32(H, W), f32(NZ, Q, W), f32(NZ, Q, W), f32(H, W),
        f32(Q, W), f32(Q, W), f32(W, W), f32(W, W),
        sem(7), sem(LOC + 2), sem(6), sem(6), sem(16), sem(16), sem(16), sem(16), sem(8), sem(8), sem(8), sem(8),
        sem(1), sem(1),
        sem(8), sem(8), sem(2), sem(2), sem(4), sem(4), sem(8), sem(8), sem(1), sem(1), sem(8), sem(8),
        sem(16), sem(16), sem(8), sem(8), sem(1), sem(1), sem(8), sem(8), sem(8), sem(8),
    ]
    solved, top = pl.pallas_call(
        kernel,
        out_shape=(
            jax.ShapeDtypeStruct((LOC + 1, W, W), F32),
            jax.ShapeDtypeStruct((TOP, W, W), F32),
        ),
        in_specs=[smem, smem, hbm, hbm, hbm, vmem, vmem, hbm, hbm, hbm, vmem, vmem],
        out_specs=(hbm, hbm),
        scratch_shapes=scratch,
        compiler_params=pltpu.CompilerParams(
            collective_id=0, has_side_effects=True, vmem_limit_bytes=56 * 1024 * 1024
        ),
    )(
        ancestors[0, 0].T,
        chain_target[0],
        node_rhs[0, 0],
        node_inverse[0, 0],
        local_blocks[0, 0].reshape(LOC, 128, W),
        chain_next[0, 0],
        chain_top[0, 0],
        top_rhs,
        top_inverse,
        top_next,
        block_rows[0, 0].reshape(2 * LOC, 64),
        chain_rows[0],
    )
    return solved[None, None], top


def solution(mesh):
    placed = (
        P("leaf", "col", None, None, None),
        P("leaf", "col", None, None, None),
        P("leaf", "col", None, None, None, None),
        P("leaf", "col", None, None),
        P("leaf", "col", None, None),
        P(),
        P(),
        P(),
        P("leaf", "col", None, None),
        P("leaf", "col", None, None, None),
        P("leaf", "col"),
        P("leaf", "col", None),
    )
    return jax.shard_map(
        shards,
        mesh=mesh,
        in_specs=placed,
        out_specs=(P("leaf", "col", None, None, None), P()),
        check_vma=False,
    )
```
